256 devices in a mesh: group: 8 (over x, y_lo), blk: 32 (over z, y_hi, core).
Axes of the slice: x: 4, y: 4 (y_hi: 2, y_lo: 2; y = y_hi * 2 + y_lo), z: 8, core: 2. Of those that a mesh axis runs over, the one named last changes fastest.
Arguments:
- img_feat: bfloat16 [131072, 1152], P(('group', 'blk')), may hold values from -6 to 6
- txt_feat: bfloat16 [131072, 1152], P(('group', 'blk')), may hold values from -6 to 6
- img_proj: bfloat16 [1152, 1152], replicated, may hold values from -0.1875 to 0.1875
- txt_proj: bfloat16 [1152, 1152], replicated, may hold values from -0.1875 to 0.1875
- pos_index: int32 [131072], P(('group', 'blk')), may hold values from 0 to 16383, as said below
- logit_scale: float32 [1], replicated, may hold values from 10 to 40
- logit_bias: float32 [1], replicated, may hold values from -3 to 0
Outputs:
- img_feat_grad: bfloat16 [131072, 1152], P(('group', 'blk'))
- txt_feat_grad: bfloat16 [131072, 1152], P(('group', 'blk'))
- img_proj_grad: float32 [1152, 1152], P('blk')
- txt_proj_grad: float32 [1152, 1152], P('blk')
The draws below stay inside these ranges and needn't reach their ends.
Inputs may be any that keep to these rules, and one draw needn't show every extreme that they name: `pos_index`: the matching text row of an image row in block k lies in block (k - o) mod (32) for some o in 0 .. 2; several image rows may match one text row.
All inputs are finite; a program needn't handle non-finite values.
Results may differ from the reference program's by a relative error of at most 0.018.
Values may be sent and summed in bfloat16 or wider, within the bound.
A program may use at most 64 MiB of HBM per device.

```python
import math
import jax
import jax.numpy as jnp
from jax import lax

D = 1152
TOK_DEV = 512
STEPS = 3
GROUP_ROWS = 16384
ROWS = 131072


def draw_pos_index(key, part):
    key = jax.random.fold_in(key, 11)
    first_key, second_key = jax.random.split(key)
    index = jnp.arange(ROWS, dtype=jnp.int32)
    nblocks = GROUP_ROWS // TOK_DEV
    block = index % GROUP_ROWS // TOK_DEV
    back = jax.random.randint(first_key, (ROWS,), 0, STEPS, dtype=jnp.int32)
    within = jax.random.randint(second_key, (ROWS,), 0, TOK_DEV, dtype=jnp.int32)
    back = back.at[0].set(1).at[1].set(0)
    within = within.at[0].set(TOK_DEV - 1).at[1].set(0)
    return ((block - back) % nblocks * TOK_DEV + within).astype(jnp.int32)


def block_scale(key, extent, cuts, smallest, largest):
    factor_of = 1.0
    for dim, blocks in cuts:
        draws = jax.random.uniform(jax.random.fold_in(jax.random.fold_in(key, 6), dim), (blocks,), jnp.float32, smallest / len(cuts), largest / len(cuts))
        factor_of = factor_of * jnp.repeat(jnp.exp(draws), extent[dim] // blocks).reshape((-1,) + (1,) * (len(extent) - 1 - dim))
    return factor_of


def centred(own_key, dims, deviation, most, shards=(), kind=jnp.bfloat16):
    array = deviation * jax.random.normal(own_key, dims, jnp.float32)
    if shards:
        array = array * block_scale(own_key, dims, shards, -0.22, 0.18)
    return jnp.clip(array, -most, most).astype(kind)


def setup_inputs(seed: int = 0) -> dict:
    seeds = jax.random.split(jax.random.key(seed), 8)
    img_feat = centred(seeds[0], (ROWS, D), 1.0, 6.0, ((0, 256),))
    txt_feat = centred(seeds[1], (ROWS, D), 1.0, 6.0, ((0, 256),))
    img_proj = centred(seeds[2], (D, D), D ** -0.5, 0.1875)
    txt_proj = centred(seeds[3], (D, D), D ** -0.5, 0.1875)
    pos_index = draw_pos_index(jax.random.fold_in(seeds[7], 71), 0)
    logit_scale = jnp.clip(jnp.exp(jax.random.uniform(seeds[5], (1,), jnp.float32, math.log(10.0), math.log(40.0))), 10.0, 40.0)
    logit_bias = jnp.clip(jax.random.uniform(seeds[6], (1,), jnp.float32, -3.0, 0.0), -3.0, 0.0)
    return dict(img_feat=img_feat, txt_feat=txt_feat, img_proj=img_proj, txt_proj=txt_proj, pos_index=pos_index, logit_scale=logit_scale, logit_bias=logit_bias)


epsilon = 1e-06

def unit_rows(features, projection):
    embedded = jnp.dot(features, projection, preferred_element_type=jnp.float32)
    inverse = lax.rsqrt(lax.optimization_barrier(jnp.sum(embedded * embedded, axis=-1, keepdims=True)) + epsilon)
    exact = embedded * inverse
    return (exact.astype(jnp.bfloat16), exact, inverse)

def norm_backward(exact, inverse, upstream):
    return inverse * (upstream - exact * lax.optimization_barrier(jnp.sum(exact * upstream, axis=-1, keepdims=True)))

def reference(img_feat, txt_feat, img_proj, txt_proj, pos_index, logit_scale, logit_bias):
    scale = logit_scale[0]
    bias = logit_bias[0]
    img_unit, img_exact, img_inverse = unit_rows(img_feat, img_proj)
    txt_unit, txt_exact, txt_inverse = unit_rows(txt_feat, txt_proj)
    nblocks = GROUP_ROWS // TOK_DEV
    ngroups = ROWS // GROUP_ROWS
    layout = (ngroups, nblocks, TOK_DEV, D)
    img_blocks = lax.optimization_barrier(img_unit).astype(jnp.float32).reshape(layout)
    txt_blocks = lax.optimization_barrier(txt_unit).astype(jnp.float32).reshape(layout)
    targets = pos_index.reshape(ngroups, nblocks, TOK_DEV)
    columns = jnp.arange(TOK_DEV, dtype=jnp.int32)
    block_ids = jnp.arange(nblocks, dtype=jnp.int32)

    def one_group(packed):
        img_group, txt_group, target_group = packed
        img_grad = jnp.zeros_like(img_group)
        txt_grad = jnp.zeros_like(txt_group)
        for offset in range(STEPS):
            visiting = jnp.roll(txt_group, offset, axis=0)
            logits = scale * jnp.einsum('kid,kjd->kij', img_group, visiting) + bias
            owner = (block_ids - offset) % nblocks
            matches = target_group[:, :, None] == (owner * TOK_DEV)[:, None, None] + columns[None, None, :]
            weights = (jax.nn.sigmoid(logits) - matches.astype(jnp.float32)).astype(jnp.bfloat16)
            weights = lax.optimization_barrier(weights).astype(jnp.float32)
            img_grad = img_grad + scale * jnp.einsum('kij,kjd->kid', weights, visiting)
            shares = scale * jnp.einsum('kij,kid->kjd', weights, img_group)
            txt_grad = txt_grad + jnp.roll(shares, -offset, axis=0)
        return (img_grad, txt_grad)
    img_grad, txt_grad = lax.map(one_group, (img_blocks, txt_blocks, targets))
    img_delta = norm_backward(img_exact, img_inverse, img_grad.reshape(ROWS, D)).astype(jnp.bfloat16)
    txt_delta = norm_backward(txt_exact, txt_inverse, txt_grad.reshape(ROWS, D)).astype(jnp.bfloat16)
    img_feat_grad = jnp.dot(img_delta, img_proj.T, preferred_element_type=jnp.float32).astype(jnp.bfloat16)
    txt_feat_grad = jnp.dot(txt_delta, txt_proj.T, preferred_element_type=jnp.float32).astype(jnp.bfloat16)

    def accumulate(total, index):
        start = (index * TOK_DEV).astype(jnp.int32)
        img_rows = lax.dynamic_slice_in_dim(img_feat, start, TOK_DEV, 0)
        txt_rows = lax.dynamic_slice_in_dim(txt_feat, start, TOK_DEV, 0)
        img_part = lax.dynamic_slice_in_dim(img_delta, start, TOK_DEV, 0)
        txt_part = lax.dynamic_slice_in_dim(txt_delta, start, TOK_DEV, 0)
        term = jnp.concatenate([jnp.dot(img_rows.T, img_part, preferred_element_type=jnp.float32), jnp.dot(txt_rows.T, txt_part, preferred_element_type=jnp.float32)], axis=1)
        term = lax.optimization_barrier(term.astype(jnp.bfloat16)).astype(jnp.float32)
        return (total + term, None)
    total, _ = lax.scan(accumulate, jnp.zeros((D, 2 * D), jnp.float32), jnp.arange(ROWS // TOK_DEV, dtype=jnp.int32))
    return (img_feat_grad, txt_feat_grad, total[:, :D], total[:, D:])
```

```python
import functools

import jax
import jax.numpy as jnp
from jax import lax
from jax.experimental import pallas as pl
from jax.experimental.pallas import tpu as pltpu
from jax.sharding import PartitionSpec as P

MESH = pl.DeviceIdType.MESH
EPSILON = 1e-06
ROWS = 512
WIDTH = 1152
HALF = 256
MSG = 128
NMSG = ROWS // MSG
TILES = WIDTH // 128
CHUNKS = ((0, 2), (2, 2), (4, 2), (6, 2), (8, 1))
NCH = len(CHUNKS)
ZROWS = 144
WIN = 48
OUT_ROWS = 36
BF16 = jnp.bfloat16
F32 = jnp.float32


def against(left, right):
    return lax.dot_general(
        left, right, (((1,), (1,)), ((), ())), preferred_element_type=F32
    )


def kernel(
    img_feat_hbm, txt_feat_hbm, img_proj_hbm, txt_proj_hbm, pos_hbm, scale_ref, bias_ref,
    img_back_hbm, txt_back_hbm, img_out, txt_out,
    img_feat, txt_feat, img_proj, txt_proj, pos,
    img_own, txt_own, img_dir, txt_dir, img_side, txt_side, pos_dir, pos_side, pos_rows,
    img_exact, txt_exact, img_inv, txt_inv, img_grad, txt_grad, weights,
    img_turned, txt_turned, img_delta, txt_delta, img_back, txt_back,
    part, r1, ra, q2, rb, q3, rz, q4, fin,
    load_sem, store_sem,
    ts_send, ts_recv, td_send, td_recv, is_send, is_recv, id_send, id_recv, pos_send, pos_recv,
    rs_send, rs_recv, self_send,
):
    group = lax.axis_index("group")
    blk = lax.axis_index("blk")
    x, y_lo = group // 2, lax.rem(group, 2)
    z, y_hi, c = blk // 4, lax.rem(blk // 2, 2), lax.rem(blk, 2)
    y = 2 * y_hi + y_lo
    quarter = 2 * y_hi + c

    def device(x, y, z, c):
        return (x * 2 + lax.rem(y, 2), z * 4 + (y // 2) * 2 + c)

    following = (group, lax.rem(blk + 2, 32))
    previous = (group, lax.rem(blk + 30, 32))
    sibling = (group, blk + 1 - 2 * c)
    root_z = x + 4 * c
    is_root = z == root_z

    def x_peer(d):
        return lax.rem(x + d, 4)

    def y_peer(d):
        return lax.rem(y + d, 4)

    def load(index, src, dst):
        return pltpu.make_async_copy(src, dst, load_sem.at[index])

    loads = [
        load(0, txt_proj_hbm, txt_proj),
        load(1, txt_feat_hbm, txt_feat),
        load(2, img_proj_hbm, img_proj),
        load(3, img_feat_hbm, img_feat),
        load(4, pos_hbm, pos.at[pl.ds(0, 8)]),
    ]
    for item in loads:
        item.start()

    barrier = pltpu.get_barrier_semaphore()

    def greet(target):
        pl.semaphore_signal(barrier, inc=1, device_id=target, device_id_type=MESH)

    greet(following)
    greet(previous)
    greet(sibling)
    for d in range(1, 4):
        greet(device(x_peer(d), y, z, c))
        greet(device(x, y_peer(d), z, c))
    source_x, source_c = lax.rem(z, 4), z // 4
    has_source = (source_x != x) | (source_c != c) | (quarter != y)

    @pl.when(has_source)
    def _():
        greet(device(source_x, quarter, z, source_c))

    @pl.when(is_root)
    def _():
        for d in range(1, 8):
            greet(device(x, y, lax.rem(z + d, 8), c))

    own_target = c == lax.rem(y, 2)
    count = 9 + jnp.where(is_root, 8 - jnp.where(own_target, 1, 0), 1)

    scale = scale_ref[0]
    bias = bias_ref[0]

    def embed(feat, proj, exact, own, inv, start):
        for n in range(3):
            exact[pl.ds(start, HALF), pl.ds(n * 384, 384)] = jnp.dot(
                feat[pl.ds(start, HALF), :], proj[:, pl.ds(n * 384, 384)],
                preferred_element_type=F32,
            )

        def rows(i, _):
            at = pl.ds(pl.multiple_of(start + i * 64, 64), 64)
            value = exact[at, :]
            inverse = lax.rsqrt(jnp.sum(value * value, axis=-1, keepdims=True) + EPSILON)
            unit = value * inverse
            exact[at, :] = unit
            own[at, :] = unit.astype(BF16)
            inv[at, :] = inverse
            return 0

        lax.fori_loop(0, HALF // 64, rows, 0)

    def message(src, dst, send, recv, index, target):
        at = pl.ds(index * MSG, MSG)
        return pltpu.make_async_remote_copy(
            src.at[at], dst.at[at], send.at[index], recv.at[index],
            device_id=target, device_id_type=MESH,
        )

    def txt_direct(index):
        return message(txt_own, txt_dir, td_send, td_recv, index, following)

    def img_direct(index):
        return message(img_own, img_dir, id_send, id_recv, index, previous)

    def txt_aside(src, index):
        return message(src, txt_side, ts_send, ts_recv, index, sibling)

    def img_aside(src, index):
        return message(src, img_side, is_send, is_recv, index, sibling)

    loads[0].wait()
    loads[1].wait()
    embed(txt_feat, txt_proj, txt_exact, txt_own, txt_inv, 0)
    pl.semaphore_wait(barrier, count)
    for index in (0, 1):
        txt_direct(index).start()

    @pl.when(c == 0)
    def _():
        for index in (0, 1):
            txt_aside(txt_own, index).start()

    embed(txt_feat, txt_proj, txt_exact, txt_own, txt_inv, HALF)
    for index in (2, 3):
        txt_direct(index).start()

    @pl.when(c == 0)
    def _():
        for index in (2, 3):
            txt_aside(txt_own, index).start()

    loads[4].wait()
    pos_ahead = pltpu.make_async_remote_copy(
        pos, pos_dir, pos_send.at[0], pos_recv.at[0], device_id=previous, device_id_type=MESH
    )
    pos_ahead.start()

    def pos_aside(src):
        return pltpu.make_async_remote_copy(
            src, pos_side, pos_send.at[1], pos_recv.at[1], device_id=sibling, device_id_type=MESH
        )

    @pl.when(c == 1)
    def _():
        pos_aside(pos).start()

    loads[2].wait()
    loads[3].wait()
    embed(img_feat, img_proj, img_exact, img_own, img_inv, 0)
    embed(img_feat, img_proj, img_exact, img_own, img_inv, HALF)

    @pl.when(c == 1)
    def _():
        for index in range(NMSG):
            img_aside(img_own, index).start()

    for h in range(2):
        row = jnp.broadcast_to(pos[h : h + 1, :], (HALF, HALF))
        pos_rows[pl.ds(h * HALF, HALF), :] = row.T

    img_grad[...] = jnp.zeros_like(img_grad)
    txt_grad[...] = jnp.zeros_like(txt_grad)

    def turn(feat, turned):
        def step(t, _):
            at = pl.ds(pl.multiple_of(t * 128, 128), 128)
            turned[at, :] = feat[:, at].T
            return 0

        lax.fori_loop(0, TILES, step, 0)

    def pair(own, other, grad, matches, h):
        def block(m, _):
            at = pl.ds(pl.multiple_of(m * HALF, HALF), HALF)
            logits = scale * against(own[at, :], other[pl.ds(h * HALF, HALF), :]) + bias
            weight = jax.nn.sigmoid(logits) - matches(m, h).astype(F32)
            weights[at, :] = weight.astype(BF16)
            return 0

        lax.fori_loop(0, 2, block, 0)

        def columns(n, _):
            at = pl.ds(pl.multiple_of(n * 384, 384), 384)
            grad[:, at] += jnp.dot(
                weights[...], other[pl.ds(h * HALF, HALF), at], preferred_element_type=F32
            )
            return 0

        lax.fori_loop(0, 3, columns, 0)

    def txt_matches(back):
        owner = lax.rem(blk - back + 32, 32)

        def matches(m, h):
            first = owner * ROWS + h * HALF
            column = first + lax.broadcasted_iota(jnp.int32, (HALF, HALF), 1)
            return pos_rows[pl.ds(pl.multiple_of(m * HALF, HALF), HALF), :] == column

        return matches

    def img_matches(pos_ref):
        def matches(m, h):
            first = blk * ROWS + m * HALF
            row = first + lax.broadcasted_iota(jnp.int32, (HALF, HALF), 0)
            return jnp.broadcast_to(pos_ref[h : h + 1, :], (HALF, HALF)) == row

        return matches

    def pair_txt(other, back, h):
        pair(img_own, other, img_grad, txt_matches(back), h)

    def pair_img(other, pos_ref, h):
        pair(txt_own, other, txt_grad, img_matches(pos_ref), h)

    for h in range(2):
        pair_txt(txt_own, 0, h)
        pair_img(img_own, pos, h)

    pos_ahead.wait_recv()

    @pl.when(c == 0)
    def _():
        pos_aside(pos_dir).start()

    pos_aside(pos).wait_recv()

    def side_txt(h):
        for index in (2 * h, 2 * h + 1):
            txt_aside(txt_own, index).wait_recv()
        pair_txt(txt_side, 1, h)

    def side_img(h):
        for index in (2 * h, 2 * h + 1):
            img_aside(img_own, index).wait_recv()
        pair_img(img_side, pos_side, h)

    @pl.when(c == 1)
    def _():
        side_txt(0)
        side_txt(1)

    @pl.when(c == 0)
    def _():
        side_img(0)
        side_img(1)

    turn(img_feat, img_turned)
    turn(txt_feat, txt_turned)

    for h in range(2):
        for index in (2 * h, 2 * h + 1):
            txt_direct(index).wait_recv()

            @pl.when(c == 1)
            def _():
                txt_aside(txt_dir, index).start()

        if h == 1:
            for index in range(NMSG):
                txt_direct(index).wait_send()
            for index in range(NMSG):
                img_direct(index).start()
        pair_txt(txt_dir, 2, h)

        @pl.when(c == 0)
        def _():
            side_txt(h)

    def finish(grad, exact, inv, delta):
        def rows(i, _):
            at = pl.ds(pl.multiple_of(i * 64, 64), 64)
            value = scale * grad[at, :]
            unit = exact[at, :]
            along = jnp.sum(unit * value, axis=-1, keepdims=True)
            delta[at, :] = (inv[at, :] * (value - unit * along)).astype(BF16)
            return 0

        lax.fori_loop(0, ROWS // 64, rows, 0)

    def waiter(ref, sem):
        return pltpu.make_async_copy(ref, ref, sem)

    class Chunk:
        def __init__(self, u, ch):
            self.u, self.ch = u, ch
            first, count = CHUNKS[ch]
            self.t = pl.ds(first, count)
            self.first, self.count = first, count

        def sem(self, stage):
            return rs_send.at[self.u, self.ch, stage], rs_recv.at[self.u, self.ch, stage]

        def copy(self, stage, src, dst, target):
            send, recv = self.sem(stage)
            pltpu.make_async_remote_copy(
                src, dst, send, recv, device_id=target, device_id_type=MESH
            ).start()

        def make(self, turned, delta):
            def block(m, _):
                at = pl.ds(pl.multiple_of(m * 288, 288), 288)
                value = jnp.dot(
                    turned[at, :], delta[:, self.first * 128 : (self.first + self.count) * 128],
                    preferred_element_type=F32,
                ).astype(BF16)
                for i in range(self.count):
                    part[self.u, self.first + i, at, :] = value[:, i * 128 : (i + 1) * 128]
                return 0

            lax.fori_loop(0, 4, block, 0)
            other = pl.ds(pl.multiple_of(576 * (1 - c), 576), 576)
            self.copy(0, part.at[self.u, self.t, other], r1.at[self.u, self.t], sibling)

        def add_core(self):
            u, t = self.u, self.t
            send, recv = self.sem(0)
            waiter(r1.at[u, t], recv).wait()

            def step(i, _):
                tile = self.first + i
                mine = pl.ds(pl.multiple_of(576 * c, 576), 576)
                r1[u, tile] = (
                    part[u, tile, mine, :].astype(F32) + r1[u, tile].astype(F32)
                ).astype(BF16)
                return 0

            lax.fori_loop(0, self.count, step, 0)
            for d in range(1, 4):
                rows = pl.ds(pl.multiple_of(ZROWS * x_peer(d), ZROWS), ZROWS)
                self.copy(
                    1, r1.at[u, t, rows], ra.at[u, d - 1, t], device(x_peer(d), y, z, c)
                )

        def add_x(self):
            u, t = self.u, self.t
            waiter(ra.at[u, :, t], self.sem(1)[1]).wait()

            def step(i, _):
                tile = self.first + i
                rows = pl.ds(pl.multiple_of(ZROWS * x, ZROWS), ZROWS)
                total = r1[u, tile, rows, :].astype(F32)
                for d in range(3):
                    total = total + ra[u, d, tile].astype(F32)
                q2[u, tile] = total.astype(BF16)
                return 0

            lax.fori_loop(0, self.count, step, 0)
            for d in range(1, 4):
                rows = pl.ds(pl.multiple_of(32 * y_peer(d), 32), WIN)
                self.copy(
                    2, q2.at[u, t, rows], rb.at[u, d - 1, t], device(x, y_peer(d), z, c)
                )

        def add_y(self):
            u, t = self.u, self.t
            waiter(rb.at[u, :, t], self.sem(2)[1]).wait()

            def step(i, _):
                tile = self.first + i
                rows = pl.ds(pl.multiple_of(32 * y, 32), WIN)
                total = q2[u, tile, rows, :].astype(F32)
                for d in range(3):
                    total = total + rb[u, d, tile].astype(F32)
                q3[u, tile] = total.astype(BF16)
                return 0

            lax.fori_loop(0, self.count, step, 0)

            @pl.when(jnp.logical_not(is_root))
            def _():
                slot = lax.rem(z - root_z + 8, 8) - 1
                self.copy(3, q3.at[u, t], rz.at[u, slot, t], device(x, y, root_z, c))

        def targets(self):
            for dx in range(4):
                for dy in range(2):
                    far_y = 2 * y_hi + lax.rem(y_lo + dy, 2)
                    yield (dx, dy), device(x_peer(dx), far_y, z, y_lo)

        def add_z(self):
            u, t = self.u, self.t

            @pl.when(is_root)
            def _():
                waiter(rz.at[u, :, t], self.sem(3)[1]).wait()

                def step(i, _):
                    tile = self.first + i
                    total = q3[u, tile].astype(F32)
                    for d in range(7):
                        total = total + rz[u, d, tile].astype(F32)
                    q4[u, tile] = total.astype(BF16)
                    return 0

                lax.fori_loop(0, self.count, step, 0)
                for where, target in self.targets():
                    if where != (0, 0):
                        self.copy(4, q4.at[u, t], fin.at[u, t], target)
                    else:

                        @pl.when(own_target)
                        def _():
                            pltpu.make_async_copy(
                                q4.at[u, t], fin.at[u, t], self.sem(4)[1]
                            ).start()

                        @pl.when(jnp.logical_not(own_target))
                        def _():
                            pltpu.make_async_remote_copy(
                                q4.at[u, t], fin.at[u, t],
                                self_send.at[u, self.ch], self.sem(4)[1],
                                device_id=target, device_id_type=MESH,
                            ).start()

        def collect(self, out):
            u = self.u
            waiter(fin.at[u, self.t], self.sem(4)[1]).wait()
            for q in range(4):

                @pl.when(quarter == q)
                def _():
                    for i in range(self.count):
                        tile = self.first + i
                        out[:, tile * 128 : (tile + 1) * 128] = fin[u, tile].astype(F32)[
                            4 * q : 4 * q + OUT_ROWS
                        ]

        def drain(self):
            u, t = self.u, self.t
            waiter(r1.at[u, t], self.sem(0)[0]).wait()
            waiter(ra.at[u, :, t], self.sem(1)[0]).wait()
            waiter(rb.at[u, :, t], self.sem(2)[0]).wait()

            @pl.when(jnp.logical_not(is_root))
            def _():
                waiter(q3.at[u, t], self.sem(3)[0]).wait()

            @pl.when(is_root)
            def _():
                waiter(rz.at[u, :, t], self.sem(4)[0]).wait()

                @pl.when(jnp.logical_not(own_target))
                def _():
                    waiter(q4.at[u, t], self_send.at[u, self.ch]).wait()

    img_chunks = [Chunk(0, ch) for ch in range(NCH)]
    txt_chunks = [Chunk(1, ch) for ch in range(NCH)]

    def back(delta, proj, staged, out, index):
        def columns(n, _):
            at = pl.ds(pl.multiple_of(n * 384, 384), 384)
            staged[:, at] = against(delta[...], proj[at, :]).astype(BF16)
            return 0

        lax.fori_loop(0, 3, columns, 0)
        copy = pltpu.make_async_copy(staged, out, store_sem.at[index])
        copy.start()
        return copy

    finish(img_grad, img_exact, img_inv, img_delta)
    for chunk in img_chunks:
        chunk.make(img_turned, img_delta)
    for chunk in img_chunks:
        chunk.add_core()
    img_store = back(img_delta, img_proj, img_back, img_back_hbm, 0)

    for h in range(2):
        for index in (2 * h, 2 * h + 1):
            img_direct(index).wait_recv()

            @pl.when(c == 0)
            def _():
                img_aside(img_dir, index).start()

        pair_img(img_dir, pos_dir, h)

        @pl.when(c == 1)
        def _():
            side_img(h)

        if h == 0:
            for chunk in img_chunks[:2]:
                chunk.add_x()

    finish(txt_grad, txt_exact, txt_inv, txt_delta)
    for chunk in txt_chunks:
        chunk.make(txt_turned, txt_delta)
    for chunk in img_chunks[2:]:
        chunk.add_x()
    for chunk in txt_chunks:
        chunk.add_core()
    for chunk in img_chunks:
        chunk.add_y()
    for chunk in img_chunks:
        chunk.add_z()
    txt_store = back(txt_delta, txt_proj, txt_back, txt_back_hbm, 1)
    for chunk in txt_chunks:
        chunk.add_x()
    for chunk in txt_chunks:
        chunk.add_y()
    for chunk in txt_chunks:
        chunk.add_z()
    for chunk in img_chunks:
        chunk.collect(img_out)
    for chunk in txt_chunks:
        chunk.collect(txt_out)

    img_store.wait()
    txt_store.wait()
    for chunk in img_chunks + txt_chunks:
        chunk.drain()
    for index in range(NMSG):
        img_direct(index).wait_send()
        txt_aside(txt_own, index).wait_send()
        img_aside(img_own, index).wait_send()
    pos_ahead.wait_send()
    pos_aside(pos).wait_send()


def per_device(img_feat, txt_feat, img_proj, txt_proj, pos_index, logit_scale, logit_bias):
    pos = jnp.pad(pos_index.reshape(2, HALF), ((0, 6), (0, 0)))
    anywhere = pl.BlockSpec(memory_space=pl.ANY)
    scalar = pl.BlockSpec(memory_space=pltpu.SMEM)
    vmem = pl.BlockSpec(memory_space=pltpu.VMEM)
    block16 = pltpu.VMEM((ROWS, WIDTH), BF16)
    block32 = pltpu.VMEM((ROWS, WIDTH), F32)
    square = pltpu.VMEM((WIDTH, WIDTH), BF16)
    places = pltpu.VMEM((8, HALF), jnp.int32)
    dma = pltpu.SemaphoreType.DMA
    return pl.pallas_call(
        kernel,
        name="pairwise",
        out_shape=(
            jax.ShapeDtypeStruct((ROWS, WIDTH), BF16),
            jax.ShapeDtypeStruct((ROWS, WIDTH), BF16),
            jax.ShapeDtypeStruct((OUT_ROWS, WIDTH), F32),
            jax.ShapeDtypeStruct((OUT_ROWS, WIDTH), F32),
        ),
        in_specs=[anywhere] * 5 + [scalar] * 2,
        out_specs=(anywhere, anywhere, vmem, vmem),
        scratch_shapes=[
            block16, block16, square, square, places,
            block16, block16, block16, block16, block16, block16, places, places,
            pltpu.VMEM((ROWS, HALF), jnp.int32),
            block32, block32, pltpu.VMEM((ROWS, 1), F32), pltpu.VMEM((ROWS, 1), F32),
            block32, block32, pltpu.VMEM((ROWS, HALF), BF16),
            pltpu.VMEM((WIDTH, ROWS), BF16), pltpu.VMEM((WIDTH, ROWS), BF16),
            block16, block16, block16, block16,
            pltpu.VMEM((2, TILES, WIDTH, 128), BF16),
            pltpu.VMEM((2, TILES, WIDTH // 2, 128), BF16),
            pltpu.VMEM((2, 3, TILES, ZROWS, 128), BF16),
            pltpu.VMEM((2, TILES, ZROWS, 128), BF16),
            pltpu.VMEM((2, 3, TILES, WIN, 128), BF16),
            pltpu.VMEM((2, TILES, WIN, 128), BF16),
            pltpu.VMEM((2, 7, TILES, WIN, 128), BF16),
            pltpu.VMEM((2, TILES, WIN, 128), BF16),
            pltpu.VMEM((2, TILES, WIN, 128), BF16),
            dma((5,)), dma((2,)),
            dma((NMSG,)), dma((NMSG,)), dma((NMSG,)), dma((NMSG,)),
            dma((NMSG,)), dma((NMSG,)), dma((NMSG,)), dma((NMSG,)),
            dma((2,)), dma((2,)),
            dma((2, NCH, 5)), dma((2, NCH, 5)), dma((2, NCH)),
        ],
        compiler_params=pltpu.CompilerParams(
            collective_id=0, has_side_effects=True, vmem_limit_bytes=62 * 1024 * 1024
        ),
        cost_estimate=pl.CostEstimate(
            flops=15_000_000_000, bytes_accessed=12_000_000, transcendentals=1_500_000
        ),
    )(img_feat, txt_feat, img_proj, txt_proj, pos, logit_scale, logit_bias)


def solution(mesh):
    both = P(("group", "blk"), None)
    in_specs = (both, both, P(), P(), P(("group", "blk")), P(), P())
    out_specs = (both, both, P("blk", None), P("blk", None))
    return jax.shard_map(
        per_device, mesh=mesh, in_specs=in_specs, out_specs=out_specs, check_vma=False
    )
```

```python
import functools

import jax
import jax.numpy as jnp
from jax import lax
from jax.experimental import pallas as pl
from jax.experimental.pallas import tpu as pltpu
from jax.sharding import PartitionSpec as P

MESH = pl.DeviceIdType.MESH
EPSILON = 1e-06
ROWS = 512
WIDTH = 1152
HALF = 256
STEP = 128
MSG = 64
NMSG = ROWS // MSG
PER_STEP = STEP // MSG
TILES = WIDTH // 128
CHUNKS = ((0, 2), (2, 2), (4, 2), (6, 2), (8, 1))
ORDERS = ("xxxxx", "xyxyx")
COLUMNS = tuple((n, min(256, WIDTH - n)) for n in range(0, WIDTH, 256))
NCH = len(CHUNKS)
ZROWS = 144
WIN = 48
OUT_ROWS = 36
BF16 = jnp.bfloat16
F32 = jnp.float32


def against(left, right):
    return lax.dot_general(
        left, right, (((1,), (1,)), ((), ())), preferred_element_type=F32
    )


def kernel(
    img_feat_hbm, txt_feat_hbm, img_proj_hbm, txt_proj_hbm, pos_hbm, scale_ref, bias_ref,
    img_back_hbm, txt_back_hbm, img_out, txt_out,
    img_feat, txt_feat, img_proj, txt_proj, pos,
    img_own, txt_own, img_dir, txt_dir, img_side, txt_side, pos_dir, pos_side, pos_rows,
    img_exact, txt_exact, img_inv, txt_inv, img_grad, txt_grad, weights,
    img_delta, txt_delta, img_back, txt_back,
    part, r1, ra, q2, rb, q3, rz, q4, fin,
    load_sem, store_sem,
    ts_send, ts_recv, td_send, td_recv, is_send, is_recv, id_send, id_recv, pos_send, pos_recv,
    rs_send, rs_recv, self_send, turn_sem,
):
    group = lax.axis_index("group")
    blk = lax.axis_index("blk")
    x, y_lo = group // 2, lax.rem(group, 2)
    z, y_hi, c = blk // 4, lax.rem(blk // 2, 2), lax.rem(blk, 2)
    y = 2 * y_hi + y_lo
    quarter = 2 * y_hi + c

    def device(x, y, z, c):
        return (x * 2 + lax.rem(y, 2), z * 4 + (y // 2) * 2 + c)

    following = (group, lax.rem(blk + 2, 32))
    previous = (group, lax.rem(blk + 30, 32))
    sibling = (group, blk + 1 - 2 * c)
    root_z = {"x": x + 4 * c, "y": y + 4 * c}
    is_root = {order: z == root_z[order] for order in "xy"}
    window = {"x": y, "y": x}
    own_target = {
        order: (y_hi == window[order] // 2) & (c == lax.rem(window[order], 2)) for order in "xy"
    }

    def x_peer(d):
        return lax.rem(x + d, 4)

    def y_peer(d):
        return lax.rem(y + d, 4)

    def load(index, src, dst):
        return pltpu.make_async_copy(src, dst, load_sem.at[index])

    loads = [
        load(0, txt_proj_hbm, txt_proj),
        load(1, txt_feat_hbm, txt_feat),
        load(2, img_proj_hbm, img_proj),
        load(3, img_feat_hbm, img_feat),
        load(4, pos_hbm, pos),
    ]
    for item in loads:
        item.start()

    barrier = pltpu.get_barrier_semaphore()

    def greet(target):
        pl.semaphore_signal(barrier, inc=1, device_id=target, device_id_type=MESH)

    greet(following)
    greet(previous)
    greet(sibling)
    for d in range(1, 4):
        greet(device(x_peer(d), y, z, c))
        greet(device(x, y_peer(d), z, c))
    sources = {
        "x": device(lax.rem(z, 4), quarter, z, z // 4),
        "y": device(quarter, lax.rem(z, 4), z, z // 4),
    }
    count = 9
    for order in "xy":
        source = sources[order]

        @pl.when((source[0] != group) | (source[1] != blk))
        def _():
            greet(source)

        @pl.when(is_root[order])
        def _():
            for d in range(1, 8):
                greet(device(x, y, lax.rem(z + d, 8), c))

        count = count + jnp.where(is_root[order], 8 - jnp.where(own_target[order], 1, 0), 1)

    scale = scale_ref[0]
    bias = bias_ref[0]

    def embed(feat, proj, exact, own, inv, start):
        for n, wide in COLUMNS:
            exact[start : start + STEP, n : n + wide] = jnp.dot(
                feat[start : start + STEP, :], proj[:, n : n + wide], preferred_element_type=F32
            )
        for i in range(STEP // 64):
            at = pl.ds(start + i * 64, 64)
            value = exact[at, :]
            inverse = lax.rsqrt(jnp.sum(value * value, axis=-1, keepdims=True) + EPSILON)
            unit = value * inverse
            exact[at, :] = unit
            own[at, :] = unit.astype(BF16)
            inv[at, :] = inverse

    def message(src, dst, send, recv, index, target):
        at = pl.ds(index * MSG, MSG)
        return pltpu.make_async_remote_copy(
            src.at[at], dst.at[at], send.at[index], recv.at[index],
            device_id=target, device_id_type=MESH,
        )

    def txt_direct(index):
        return message(txt_own, txt_dir, td_send, td_recv, index, following)

    def img_direct(index):
        return message(img_own, img_dir, id_send, id_recv, index, previous)

    def txt_aside(src, index):
        return message(src, txt_side, ts_send, ts_recv, index, sibling)

    def img_aside(src, index):
        return message(src, img_side, is_send, is_recv, index, sibling)

    loads[0].wait()
    loads[1].wait()
    for step in range(ROWS // STEP):
        embed(txt_feat, txt_proj, txt_exact, txt_own, txt_inv, step * STEP)
        if step == 0:
            pl.semaphore_wait(barrier, count)
        for index in range(step * PER_STEP, (step + 1) * PER_STEP):
            txt_direct(index).start()

            @pl.when(c == 0)
            def _():
                txt_aside(txt_own, index).start()

    loads[4].wait()
    pos_ahead = pltpu.make_async_remote_copy(
        pos, pos_dir, pos_send.at[0], pos_recv.at[0], device_id=previous, device_id_type=MESH
    )
    pos_ahead.start()

    def pos_aside(src):
        return pltpu.make_async_remote_copy(
            src, pos_side, pos_send.at[1], pos_recv.at[1], device_id=sibling, device_id_type=MESH
        )

    @pl.when(c == 1)
    def _():
        pos_aside(pos).start()

    loads[2].wait()
    loads[3].wait()
    for step in range(ROWS // STEP):
        embed(img_feat, img_proj, img_exact, img_own, img_inv, step * STEP)

    @pl.when(c == 1)
    def _():
        for index in range(NMSG):
            img_aside(img_own, index).start()

    def pos_row(pos_ref, first, many):
        return jnp.concatenate([pos_ref[first + i : first + i + 1, :] for i in range(many)], axis=1)

    for h in range(2):
        row = jnp.broadcast_to(pos_row(pos, 2 * h, 2), (HALF, HALF))
        pos_rows[pl.ds(h * HALF, HALF), :] = row.T

    def pair(own, other, grad, matches, start, many, fresh=False):
        logits = scale * against(own[...], other[start : start + many, :]) + bias
        weight = jax.nn.sigmoid(logits) - matches(start, many).astype(F32)
        weights[:, :many] = weight.astype(BF16)
        for n, wide in COLUMNS:
            product = jnp.dot(
                weights[:, :many], other[start : start + many, n : n + wide],
                preferred_element_type=F32,
            )
            if fresh:
                grad[:, n : n + wide] = product
            else:
                grad[:, n : n + wide] += product

    def txt_matches(back):
        owner = lax.rem(blk - back + 32, 32)

        def matches(start, many):
            first = owner * ROWS + start
            column = first + lax.broadcasted_iota(jnp.int32, (ROWS, many), 1)
            mine = pos_rows[...]
            if many > HALF:
                mine = jnp.concatenate([mine, mine], axis=1)
            return mine == column

        return matches

    def img_matches(pos_ref):
        def matches(start, many):
            row = blk * ROWS + lax.broadcasted_iota(jnp.int32, (ROWS, many), 0)
            mine = pos_row(pos_ref, start // 128, many // 128)
            return jnp.broadcast_to(mine, (ROWS, many)) == row

        return matches

    def pair_txt(other, back, start, many, fresh=False):
        pair(img_own, other, img_grad, txt_matches(back), start, many, fresh)

    def pair_img(other, pos_ref, start, many, fresh=False):
        pair(txt_own, other, txt_grad, img_matches(pos_ref), start, many, fresh)

    pair_txt(txt_own, 0, 0, ROWS, fresh=True)
    pair_img(img_own, pos, 0, ROWS, fresh=True)

    pos_ahead.wait_recv()

    @pl.when(c == 0)
    def _():
        pos_aside(pos_dir).start()

    pos_aside(pos).wait_recv()

    def side_txt(start, many):
        for index in range(start // MSG, (start + many) // MSG):
            txt_aside(txt_own, index).wait_recv()
        pair_txt(txt_side, 1, start, many)

    def side_img(start, many):
        for index in range(start // MSG, (start + many) // MSG):
            img_aside(img_own, index).wait_recv()
        pair_img(img_side, pos_side, start, many)

    @pl.when(c == 1)
    def _():
        side_txt(0, ROWS)

    @pl.when(c == 0)
    def _():
        side_img(0, ROWS)

    for h in range(2):
        for index in range(h * HALF // MSG, (h + 1) * HALF // MSG):
            txt_direct(index).wait_recv()

            @pl.when(c == 1)
            def _():
                txt_aside(txt_dir, index).start()

        if h == 1:
            for index in range(NMSG):
                txt_direct(index).wait_send()
            for d in range(1, 4):
                pl.semaphore_signal(
                    turn_sem, inc=1, device_id=device(x, y_peer(d), z, c), device_id_type=MESH
                )
            pl.semaphore_signal(turn_sem, inc=1, device_id=sibling, device_id_type=MESH)
            pl.semaphore_wait(turn_sem, 4)
            for index in range(NMSG):
                img_direct(index).start()
        pair_txt(txt_dir, 2, h * HALF, HALF)

        @pl.when(c == 0)
        def _():
            side_txt(h * HALF, HALF)

    def finish(grad, exact, inv, delta):
        def rows(i, _):
            for j in range(4):
                at = pl.ds(pl.multiple_of(i * 128 + j * 32, 32), 32)
                value = scale * grad[at, :]
                unit = exact[at, :]
                along = jnp.sum(unit * value, axis=-1, keepdims=True)
                delta[at, :] = (inv[at, :] * (value - unit * along)).astype(BF16)
            return 0

        lax.fori_loop(0, ROWS // 128, rows, 0)

    def waiter(ref, sem):
        return pltpu.make_async_copy(ref, ref, sem)

    class Chunk:
        def __init__(self, u, ch):
            self.u, self.ch = u, ch
            first, count = CHUNKS[ch]
            self.t = pl.ds(first, count)
            self.first, self.count = first, count
            order = ORDERS[u][ch]
            self.order = order
            self.is_root, self.own_target = is_root[order], own_target[order]
            self.near = x if order == "x" else y
            self.far = window[order]

        def near_peer(self, d):
            if self.order == "x":
                return x_peer(d), device(x_peer(d), y, z, c)
            return y_peer(d), device(x, y_peer(d), z, c)

        def far_peer(self, d):
            if self.order == "x":
                return y_peer(d), device(x, y_peer(d), z, c)
            return x_peer(d), device(x_peer(d), y, z, c)

        def sem(self, stage):
            return rs_send.at[self.u, self.ch, stage], rs_recv.at[self.u, self.ch, stage]

        def copy(self, stage, src, dst, target):
            send, recv = self.sem(stage)
            pltpu.make_async_remote_copy(
                src, dst, send, recv, device_id=target, device_id_type=MESH
            ).start()

        def make(self, feat, delta):
            columns = pl.ds(self.first * 128, self.count * 128)
            value = lax.dot_general(
                feat[...], delta[:, columns], (((0,), (0,)), ((), ())),
                preferred_element_type=F32,
            ).astype(BF16)
            for i in range(self.count):
                part[self.u, self.first + i] = value[:, i * 128 : (i + 1) * 128]
            other = pl.ds(pl.multiple_of(576 * (1 - c), 576), 576)
            self.copy(0, part.at[self.u, self.t, other], r1.at[self.u, self.t], sibling)

        def add_core(self):
            u, t = self.u, self.t
            send, recv = self.sem(0)
            waiter(r1.at[u, t], recv).wait()

            def step(i, _):
                tile = self.first + i
                mine = pl.ds(pl.multiple_of(576 * c, 576), 576)
                r1[u, tile] = (
                    part[u, tile, mine, :].astype(F32) + r1[u, tile].astype(F32)
                ).astype(BF16)
                return 0

            lax.fori_loop(0, self.count, step, 0)
            for d in range(1, 4):
                place, target = self.near_peer(d)
                rows = pl.ds(pl.multiple_of(ZROWS * place, ZROWS), ZROWS)
                self.copy(1, r1.at[u, t, rows], ra.at[u, d - 1, t], target)

        def add_near(self):
            u, t = self.u, self.t
            waiter(ra.at[u, :, t], self.sem(1)[1]).wait()

            def step(i, _):
                tile = self.first + i
                rows = pl.ds(pl.multiple_of(ZROWS * self.near, ZROWS), ZROWS)
                total = r1[u, tile, rows, :].astype(F32)
                for d in range(3):
                    total = total + ra[u, d, tile].astype(F32)
                q2[u, tile] = total.astype(BF16)
                return 0

            lax.fori_loop(0, self.count, step, 0)
            for d in range(1, 4):
                place, target = self.far_peer(d)
                rows = pl.ds(pl.multiple_of(32 * place, 32), WIN)
                self.copy(2, q2.at[u, t, rows], rb.at[u, d - 1, t], target)

        def add_far(self):
            u, t = self.u, self.t
            waiter(rb.at[u, :, t], self.sem(2)[1]).wait()

            def step(i, _):
                tile = self.first + i
                rows = pl.ds(pl.multiple_of(32 * self.far, 32), WIN)
                total = q2[u, tile, rows, :].astype(F32)
                for d in range(3):
                    total = total + rb[u, d, tile].astype(F32)
                q3[u, tile] = total.astype(BF16)
                return 0

            lax.fori_loop(0, self.count, step, 0)

            @pl.when(jnp.logical_not(self.is_root))
            def _():
                far_z = root_z[self.order]
                slot = lax.rem(z - far_z + 8, 8) - 1
                self.copy(3, q3.at[u, t], rz.at[u, slot, t], device(x, y, far_z, c))

        def targets(self):
            for dx in range(4):
                for dy in range(2):
                    far_y = 2 * (self.far // 2) + lax.rem(y_lo + dy, 2)
                    yield (dx, dy), device(x_peer(dx), far_y, z, lax.rem(self.far, 2))

        def add_z(self):
            u, t = self.u, self.t

            @pl.when(self.is_root)
            def _():
                waiter(rz.at[u, :, t], self.sem(3)[1]).wait()

                def step(i, _):
                    tile = self.first + i
                    total = q3[u, tile].astype(F32)
                    for d in range(7):
                        total = total + rz[u, d, tile].astype(F32)
                    q4[u, tile] = total.astype(BF16)
                    return 0

                lax.fori_loop(0, self.count, step, 0)
                for where, target in self.targets():
                    if where != (0, 0):
                        self.copy(4, q4.at[u, t], fin.at[u, t], target)
                    else:

                        @pl.when(self.own_target)
                        def _():
                            pltpu.make_async_copy(
                                q4.at[u, t], fin.at[u, t], self.sem(4)[1]
                            ).start()

                        @pl.when(jnp.logical_not(self.own_target))
                        def _():
                            pltpu.make_async_remote_copy(
                                q4.at[u, t], fin.at[u, t],
                                self_send.at[u, self.ch], self.sem(4)[1],
                                device_id=target, device_id_type=MESH,
                            ).start()

        def collect(self, out):
            u = self.u
            waiter(fin.at[u, self.t], self.sem(4)[1]).wait()
            for q in range(4):

                @pl.when(quarter == q)
                def _():
                    for i in range(self.count):
                        tile = self.first + i
                        out[:, tile * 128 : (tile + 1) * 128] = fin[u, tile].astype(F32)[
                            4 * q : 4 * q + OUT_ROWS
                        ]

        def drain(self):
            u, t = self.u, self.t
            waiter(r1.at[u, t], self.sem(0)[0]).wait()
            waiter(ra.at[u, :, t], self.sem(1)[0]).wait()
            waiter(rb.at[u, :, t], self.sem(2)[0]).wait()

            @pl.when(jnp.logical_not(self.is_root))
            def _():
                waiter(q3.at[u, t], self.sem(3)[0]).wait()

            @pl.when(self.is_root)
            def _():
                waiter(rz.at[u, :, t], self.sem(4)[0]).wait()

                @pl.when(jnp.logical_not(self.own_target))
                def _():
                    waiter(q4.at[u, t], self_send.at[u, self.ch]).wait()

    img_chunks = [Chunk(0, ch) for ch in range(NCH)]
    txt_chunks = [Chunk(1, ch) for ch in range(NCH)]

    def back(delta, proj, staged, out, index):
        for n, wide in COLUMNS:
            staged[:, n : n + wide] = against(delta[...], proj[n : n + wide, :]).astype(BF16)
        copy = pltpu.make_async_copy(staged, out, store_sem.at[index])
        copy.start()
        return copy

    finish(img_grad, img_exact, img_inv, img_delta)
    for chunk in img_chunks:
        chunk.make(img_feat, img_delta)
    for chunk in img_chunks:
        chunk.add_core()
    img_store = back(img_delta, img_proj, img_back, img_back_hbm, 0)

    for h in range(2):
        for index in range(h * HALF // MSG, (h + 1) * HALF // MSG):
            img_direct(index).wait_recv()

            @pl.when(c == 0)
            def _():
                img_aside(img_dir, index).start()

        pair_img(img_dir, pos_dir, h * HALF, HALF)

        @pl.when(c == 1)
        def _():
            side_img(h * HALF, HALF)

        if h == 0:
            for chunk in img_chunks:
                chunk.add_near()

    finish(txt_grad, txt_exact, txt_inv, txt_delta)
    for chunk in txt_chunks:
        chunk.make(txt_feat, txt_delta)
    for chunk in img_chunks:
        chunk.add_far()
    for chunk in txt_chunks:
        chunk.add_core()
    txt_store = back(txt_delta, txt_proj, txt_back, txt_back_hbm, 1)
    for chunk in img_chunks:
        chunk.add_z()
    for chunk in txt_chunks:
        chunk.add_near()
    for chunk in txt_chunks:
        chunk.add_far()
    for chunk in img_chunks:
        chunk.collect(img_out)
    for chunk in txt_chunks:
        chunk.add_z()
    for chunk in txt_chunks:
        chunk.collect(txt_out)

    img_store.wait()
    txt_store.wait()
    for chunk in img_chunks + txt_chunks:
        chunk.drain()
    for index in range(NMSG):
        img_direct(index).wait_send()
        txt_aside(txt_own, index).wait_send()
        img_aside(img_own, index).wait_send()
    pos_ahead.wait_send()
    pos_aside(pos).wait_send()


def deliver(*refs):
    sources, targets, held, load_sem, store_sem = refs[:4], refs[4:8], refs[8:12], refs[12], refs[13]
    loads = [
        pltpu.make_async_copy(sources[i], held[i], load_sem.at[i]) for i in range(4)
    ]
    stores = [
        pltpu.make_async_copy(held[i], targets[i], store_sem.at[i]) for i in range(4)
    ]
    for load in loads:
        load.start()
    for load, store in zip(loads, stores):
        load.wait()
        store.start()
    for store in stores:
        store.wait()


def per_device(img_feat, txt_feat, img_proj, txt_proj, pos_index, logit_scale, logit_bias):
    pos = pos_index.reshape(4, 128)
    anywhere = pl.BlockSpec(memory_space=pl.ANY)
    scalar = pl.BlockSpec(memory_space=pltpu.SMEM)
    vmem = pl.BlockSpec(memory_space=pltpu.VMEM)
    block16 = pltpu.VMEM((ROWS, WIDTH), BF16)
    block32 = pltpu.VMEM((ROWS, WIDTH), F32)
    square = pltpu.VMEM((WIDTH, WIDTH), BF16)
    places = pltpu.VMEM((4, 128), jnp.int32)
    dma = pltpu.SemaphoreType.DMA
    results = pl.pallas_call(
        kernel,
        name="pairwise",
        out_shape=(
            jax.ShapeDtypeStruct((ROWS, WIDTH), BF16),
            jax.ShapeDtypeStruct((ROWS, WIDTH), BF16),
            jax.ShapeDtypeStruct((OUT_ROWS, WIDTH), F32),
            jax.ShapeDtypeStruct((OUT_ROWS, WIDTH), F32),
        ),
        in_specs=[anywhere] * 5 + [scalar] * 2,
        out_specs=(anywhere, anywhere, vmem, vmem),
        scratch_shapes=[
            block16, block16, square, square, places,
            block16, block16, block16, block16, block16, block16, places, places,
            pltpu.VMEM((ROWS, HALF), jnp.int32),
            block32, block32, pltpu.VMEM((ROWS, 1), F32), pltpu.VMEM((ROWS, 1), F32),
            block32, block32, pltpu.VMEM((ROWS, ROWS), BF16),
            block16, block16, block16, block16,
            pltpu.VMEM((2, TILES, WIDTH, 128), BF16),
            pltpu.VMEM((2, TILES, WIDTH // 2, 128), BF16),
            pltpu.VMEM((2, 3, TILES, ZROWS, 128), BF16),
            pltpu.VMEM((2, TILES, ZROWS, 128), BF16),
            pltpu.VMEM((2, 3, TILES, WIN, 128), BF16),
            pltpu.VMEM((2, TILES, WIN, 128), BF16),
            pltpu.VMEM((2, 7, TILES, WIN, 128), BF16),
            pltpu.VMEM((2, TILES, WIN, 128), BF16),
            pltpu.VMEM((2, TILES, WIN, 128), BF16),
            dma((5,)), dma((2,)),
            dma((NMSG,)), dma((NMSG,)), dma((NMSG,)), dma((NMSG,)),
            dma((NMSG,)), dma((NMSG,)), dma((NMSG,)), dma((NMSG,)),
            dma((2,)), dma((2,)),
            dma((2, NCH, 5)), dma((2, NCH, 5)), dma((2, NCH)),
            pltpu.SemaphoreType.REGULAR,
        ],
        compiler_params=pltpu.CompilerParams(
            collective_id=0, has_side_effects=True, vmem_limit_bytes=62 * 1024 * 1024
        ),
        cost_estimate=pl.CostEstimate(
            flops=15_000_000_000, bytes_accessed=12_000_000, transcendentals=1_500_000
        ),
    )(img_feat, txt_feat, img_proj, txt_proj, pos, logit_scale, logit_bias)
    return pl.pallas_call(
        deliver,
        name="deliver",
        out_shape=tuple(jax.ShapeDtypeStruct(item.shape, item.dtype) for item in results),
        in_specs=[anywhere] * 4,
        out_specs=(anywhere,) * 4,
        scratch_shapes=[pltpu.VMEM(item.shape, item.dtype) for item in results]
        + [dma((4,)), dma((4,))],
    )(*results)


def solution(mesh):
    both = P(("group", "blk"), None)
    in_specs = (both, both, P(), P(), P(("group", "blk")), P(), P())
    out_specs = (both, both, P("blk", None), P("blk", None))
    return jax.shard_map(
        per_device, mesh=mesh, in_specs=in_specs, out_specs=out_specs, check_vma=False
    )
```

```python
import functools

import jax
import jax.numpy as jnp
from jax import lax
from jax.experimental import pallas as pl
from jax.experimental.pallas import tpu as pltpu
from jax.sharding import PartitionSpec as P

MESH = pl.DeviceIdType.MESH
EPSILON = 1e-06
ROWS = 512
WIDTH = 1152
HALF = 256
STEP = 128
MSG = 64
NMSG = ROWS // MSG
PER_STEP = STEP // MSG
TILES = WIDTH // 128
CHUNKS = ((0, 2), (2, 2), (4, 2), (6, 2), (8, 1))
ORDERS = ("x", "m")
COLUMNS = tuple((n, min(256, WIDTH - n)) for n in range(0, WIDTH, 256))
NCH = len(CHUNKS)
ZROWS = 144
WIN = 48
OUT_ROWS = 36
BF16 = jnp.bfloat16
F32 = jnp.float32


def against(left, right):
    return lax.dot_general(
        left, right, (((1,), (1,)), ((), ())), preferred_element_type=F32
    )


def kernel(
    img_feat_hbm, txt_feat_hbm, img_proj_hbm, txt_proj_hbm, pos_hbm, scale_ref, bias_ref,
    img_back_hbm, txt_back_hbm, img_out, txt_out,
    img_feat, txt_feat, img_proj, txt_proj, pos,
    img_own, txt_own, img_dir, txt_dir, img_side, txt_side, pos_dir, pos_side, pos_rows,
    img_exact, txt_exact, img_inv, txt_inv, img_grad, txt_grad, weights,
    img_delta, txt_delta, img_back, txt_back,
    part, r1, ra, q2, rb, q3, rz, q4, fin,
    load_sem, store_sem,
    ts_send, ts_recv, td_send, td_recv, is_send, is_recv, id_send, id_recv, pos_send, pos_recv,
    rs_send, rs_recv, self_send, turn_sem,
):
    group = lax.axis_index("group")
    blk = lax.axis_index("blk")
    x, y_lo = group // 2, lax.rem(group, 2)
    z, y_hi, c = blk // 4, lax.rem(blk // 2, 2), lax.rem(blk, 2)
    y = 2 * y_hi + y_lo
    quarter = 2 * y_hi + c

    def device(x, y, z, c):
        return (x * 2 + lax.rem(y, 2), z * 4 + (y // 2) * 2 + c)

    following = (group, lax.rem(blk + 2, 32))
    previous = (group, lax.rem(blk + 30, 32))
    sibling = (group, blk + 1 - 2 * c)
    root_z = {"x": x + 4 * c, "y": y + 4 * c}
    is_root = {order: z == root_z[order] for order in "xy"}
    window = {"x": y, "y": x}
    own_target = {
        order: (y_hi == window[order] // 2) & (c == lax.rem(window[order], 2)) for order in "xy"
    }

    def x_peer(d):
        return lax.rem(x + d, 4)

    def y_peer(d):
        return lax.rem(y + d, 4)

    def load(index, src, dst):
        return pltpu.make_async_copy(src, dst, load_sem.at[index])

    loads = [
        load(0, txt_proj_hbm, txt_proj),
        load(1, txt_feat_hbm, txt_feat),
        load(2, img_proj_hbm, img_proj),
        load(3, img_feat_hbm, img_feat),
        load(4, pos_hbm, pos),
    ]
    for item in loads[:2]:
        item.start()

    barrier = pltpu.get_barrier_semaphore()

    def greet(target):
        pl.semaphore_signal(barrier, inc=1, device_id=target, device_id_type=MESH)

    greet(following)
    greet(previous)
    greet(sibling)
    for d in range(1, 4):
        greet(device(x_peer(d), y, z, c))
        greet(device(x, y_peer(d), z, c))
    sources = {
        "x": device(lax.rem(z, 4), quarter, z, z // 4),
        "y": device(quarter, lax.rem(z, 4), z, z // 4),
    }
    count = 9
    for order in "xy":
        source = sources[order]

        @pl.when((source[0] != group) | (source[1] != blk))
        def _():
            greet(source)

        @pl.when(is_root[order])
        def _():
            for d in range(1, 8):
                greet(device(x, y, lax.rem(z + d, 8), c))

        count = count + jnp.where(is_root[order], 8 - jnp.where(own_target[order], 1, 0), 1)

    scale = scale_ref[0]
    bias = bias_ref[0]

    def embed(feat, proj, exact, own, inv, start):
        for n, wide in COLUMNS:
            exact[start : start + STEP, n : n + wide] = jnp.dot(
                feat[start : start + STEP, :], proj[:, n : n + wide], preferred_element_type=F32
            )
        for i in range(STEP // 64):
            at = pl.ds(start + i * 64, 64)
            value = exact[at, :]
            inverse = lax.rsqrt(jnp.sum(value * value, axis=-1, keepdims=True) + EPSILON)
            unit = value * inverse
            exact[at, :] = unit
            own[at, :] = unit.astype(BF16)
            inv[at, :] = inverse

    def message(src, dst, send, recv, index, target):
        at = pl.ds(index * MSG, MSG)
        return pltpu.make_async_remote_copy(
            src.at[at], dst.at[at], send.at[index], recv.at[index],
            device_id=target, device_id_type=MESH,
        )

    def txt_direct(index):
        return message(txt_own, txt_dir, td_send, td_recv, index, following)

    def img_direct(index):
        return message(img_own, img_dir, id_send, id_recv, index, previous)

    def txt_aside(src, index):
        return message(src, txt_side, ts_send, ts_recv, index, sibling)

    def img_aside(src, index):
        return message(src, img_side, is_send, is_recv, index, sibling)

    loads[0].wait()
    loads[1].wait()
    for item in loads[2:]:
        item.start()
    for step in range(ROWS // STEP):
        embed(txt_feat, txt_proj, txt_exact, txt_own, txt_inv, step * STEP)
        if step == 0:
            pl.semaphore_wait(barrier, count)
        for index in range(step * PER_STEP, (step + 1) * PER_STEP):
            txt_direct(index).start()

            @pl.when(c == 0)
            def _():
                txt_aside(txt_own, index).start()

    loads[4].wait()
    pos_ahead = pltpu.make_async_remote_copy(
        pos, pos_dir, pos_send.at[0], pos_recv.at[0], device_id=previous, device_id_type=MESH
    )
    pos_ahead.start()

    def pos_aside(src):
        return pltpu.make_async_remote_copy(
            src, pos_side, pos_send.at[1], pos_recv.at[1], device_id=sibling, device_id_type=MESH
        )

    @pl.when(c == 1)
    def _():
        pos_aside(pos).start()

    loads[2].wait()
    loads[3].wait()
    for step in range(ROWS // STEP):
        embed(img_feat, img_proj, img_exact, img_own, img_inv, step * STEP)

    @pl.when(c == 1)
    def _():
        for index in range(NMSG):
            img_aside(img_own, index).start()

    def pos_row(pos_ref, first, many):
        return jnp.concatenate([pos_ref[first + i : first + i + 1, :] for i in range(many)], axis=1)

    for h in range(2):
        row = jnp.broadcast_to(pos_row(pos, 2 * h, 2), (HALF, HALF))
        pos_rows[pl.ds(h * HALF, HALF), :] = row.T

    def pair(own, other, grad, matches, start, many, fresh=False):
        logits = scale * against(own[...], other[start : start + many, :]) + bias
        weight = jax.nn.sigmoid(logits) - matches(start, many).astype(F32)
        weights[:, :many] = weight.astype(BF16)
        for n, wide in COLUMNS:
            product = jnp.dot(
                weights[:, :many], other[start : start + many, n : n + wide],
                preferred_element_type=F32,
            )
            if fresh:
                grad[:, n : n + wide] = product
            else:
                grad[:, n : n + wide] += product

    def txt_matches(back):
        owner = lax.rem(blk - back + 32, 32)

        def matches(start, many):
            first = owner * ROWS + start
            column = first + lax.broadcasted_iota(jnp.int32, (ROWS, many), 1)
            mine = pos_rows[...]
            if many > HALF:
                mine = jnp.concatenate([mine, mine], axis=1)
            return mine == column

        return matches

    def img_matches(pos_ref):
        def matches(start, many):
            row = blk * ROWS + lax.broadcasted_iota(jnp.int32, (ROWS, many), 0)
            mine = pos_row(pos_ref, start // 128, many // 128)
            return jnp.broadcast_to(mine, (ROWS, many)) == row

        return matches

    def pair_txt(other, back, start, many, fresh=False):
        pair(img_own, other, img_grad, txt_matches(back), start, many, fresh)

    def pair_img(other, pos_ref, start, many, fresh=False):
        pair(txt_own, other, txt_grad, img_matches(pos_ref), start, many, fresh)

    pair_txt(txt_own, 0, 0, ROWS, fresh=True)
    pair_img(img_own, pos, 0, ROWS, fresh=True)

    pos_ahead.wait_recv()

    @pl.when(c == 0)
    def _():
        pos_aside(pos_dir).start()

    pos_aside(pos).wait_recv()

    def side_txt(start, many):
        for index in range(start // MSG, (start + many) // MSG):
            txt_aside(txt_own, index).wait_recv()
        pair_txt(txt_side, 1, start, many)

    def side_img(start, many):
        for index in range(start // MSG, (start + many) // MSG):
            img_aside(img_own, index).wait_recv()
        pair_img(img_side, pos_side, start, many)

    @pl.when(c == 1)
    def _():
        side_txt(0, ROWS)

    @pl.when(c == 0)
    def _():
        side_img(0, ROWS)

    for h in range(2):
        for index in range(h * HALF // MSG, (h + 1) * HALF // MSG):
            txt_direct(index).wait_recv()

            @pl.when(c == 1)
            def _():
                txt_aside(txt_dir, index).start()

            txt_direct(index).wait_send()
            if index == NMSG - 2:
                for d in range(1, 4):
                    pl.semaphore_signal(
                        turn_sem, inc=1, device_id=device(x, y_peer(d), z, c), device_id_type=MESH
                    )
                pl.semaphore_signal(turn_sem, inc=1, device_id=sibling, device_id_type=MESH)

        if h == 1:
            pl.semaphore_wait(turn_sem, 4)
            for index in range(NMSG):
                img_direct(index).start()
        pair_txt(txt_dir, 2, h * HALF, HALF)

        @pl.when(c == 0)
        def _():
            side_txt(h * HALF, HALF)

    def finish(grad, exact, inv, delta):
        def rows(i, _):
            for j in range(4):
                at = pl.ds(pl.multiple_of(i * 128 + j * 32, 32), 32)
                value = scale * grad[at, :]
                unit = exact[at, :]
                along = jnp.sum(unit * value, axis=-1, keepdims=True)
                delta[at, :] = (inv[at, :] * (value - unit * along)).astype(BF16)
            return 0

        lax.fori_loop(0, ROWS // 128, rows, 0)

    def waiter(ref, sem):
        return pltpu.make_async_copy(ref, ref, sem)

    class Chunk:
        def __init__(self, u, ch):
            self.u, self.ch = u, ch
            first, count = CHUNKS[ch]
            self.t = pl.ds(first, count)
            self.first, self.count = first, count
            order = ORDERS[u]
            self.along_x = (c == 0) if order == "m" else (c >= 0)
            self.is_root = self.choose(is_root["x"], is_root["y"])
            self.own_target = self.choose(own_target["x"], own_target["y"])
            self.root_z = self.choose(root_z["x"], root_z["y"])
            self.near, self.far = self.choose(x, y), self.choose(y, x)

        def choose(self, if_x, if_y):
            if if_x.dtype == jnp.bool_:
                return (self.along_x & if_x) | (jnp.logical_not(self.along_x) & if_y)
            return jnp.where(self.along_x, if_x, if_y)

        def near_peer(self, d):
            target = device(self.choose(x_peer(d), x), self.choose(y, y_peer(d)), z, c)
            return self.choose(x_peer(d), y_peer(d)), target

        def far_peer(self, d):
            target = device(self.choose(x, x_peer(d)), self.choose(y_peer(d), y), z, c)
            return self.choose(y_peer(d), x_peer(d)), target

        def sem(self, stage):
            return rs_send.at[self.u, self.ch, stage], rs_recv.at[self.u, self.ch, stage]

        def copy(self, stage, src, dst, target):
            send, recv = self.sem(stage)
            pltpu.make_async_remote_copy(
                src, dst, send, recv, device_id=target, device_id_type=MESH
            ).start()

        def make(self, feat, delta):
            columns = pl.ds(self.first * 128, self.count * 128)
            value = lax.dot_general(
                feat[...], delta[:, columns], (((0,), (0,)), ((), ())),
                preferred_element_type=F32,
            ).astype(BF16)
            for i in range(self.count):
                part[self.u, self.first + i] = value[:, i * 128 : (i + 1) * 128]
            other = pl.ds(pl.multiple_of(576 * (1 - c), 576), 576)
            self.copy(0, part.at[self.u, self.t, other], r1.at[self.u, self.t], sibling)

        def add_core(self):
            u, t = self.u, self.t
            send, recv = self.sem(0)
            waiter(r1.at[u, t], recv).wait()

            def step(i, _):
                tile = self.first + i
                mine = pl.ds(pl.multiple_of(576 * c, 576), 576)
                r1[u, tile] = (
                    part[u, tile, mine, :].astype(F32) + r1[u, tile].astype(F32)
                ).astype(BF16)
                return 0

            lax.fori_loop(0, self.count, step, 0)
            for d in range(1, 4):
                place, target = self.near_peer(d)
                rows = pl.ds(pl.multiple_of(ZROWS * place, ZROWS), ZROWS)
                self.copy(1, r1.at[u, t, rows], ra.at[u, d - 1, t], target)

        def add_near(self):
            u, t = self.u, self.t
            waiter(ra.at[u, :, t], self.sem(1)[1]).wait()

            def step(i, _):
                tile = self.first + i
                rows = pl.ds(pl.multiple_of(ZROWS * self.near, ZROWS), ZROWS)
                total = r1[u, tile, rows, :].astype(F32)
                for d in range(3):
                    total = total + ra[u, d, tile].astype(F32)
                q2[u, tile] = total.astype(BF16)
                return 0

            lax.fori_loop(0, self.count, step, 0)
            for d in range(1, 4):
                place, target = self.far_peer(d)
                rows = pl.ds(pl.multiple_of(32 * place, 32), WIN)
                self.copy(2, q2.at[u, t, rows], rb.at[u, d - 1, t], target)

        def add_far(self):
            u, t = self.u, self.t
            waiter(rb.at[u, :, t], self.sem(2)[1]).wait()

            def step(i, _):
                tile = self.first + i
                rows = pl.ds(pl.multiple_of(32 * self.far, 32), WIN)
                total = q2[u, tile, rows, :].astype(F32)
                for d in range(3):
                    total = total + rb[u, d, tile].astype(F32)
                q3[u, tile] = total.astype(BF16)
                return 0

            lax.fori_loop(0, self.count, step, 0)

            @pl.when(jnp.logical_not(self.is_root))
            def _():
                far_z = self.root_z
                slot = lax.rem(z - far_z + 8, 8) - 1
                self.copy(3, q3.at[u, t], rz.at[u, slot, t], device(x, y, far_z, c))

        def targets(self):
            for dx in range(4):
                for dy in range(2):
                    far_y = 2 * (self.far // 2) + lax.rem(y_lo + dy, 2)
                    yield (dx, dy), device(x_peer(dx), far_y, z, lax.rem(self.far, 2))

        def add_z(self):
            u, t = self.u, self.t

            @pl.when(self.is_root)
            def _():
                waiter(rz.at[u, :, t], self.sem(3)[1]).wait()

                def step(i, _):
                    tile = self.first + i
                    total = q3[u, tile].astype(F32)
                    for d in range(7):
                        total = total + rz[u, d, tile].astype(F32)
                    q4[u, tile] = total.astype(BF16)
                    return 0

                lax.fori_loop(0, self.count, step, 0)
                for where, target in self.targets():
                    if where != (0, 0):
                        self.copy(4, q4.at[u, t], fin.at[u, t], target)
                    else:

                        @pl.when(self.own_target)
                        def _():
                            pltpu.make_async_copy(
                                q4.at[u, t], fin.at[u, t], self.sem(4)[1]
                            ).start()

                        @pl.when(jnp.logical_not(self.own_target))
                        def _():
                            pltpu.make_async_remote_copy(
                                q4.at[u, t], fin.at[u, t],
                                self_send.at[u, self.ch], self.sem(4)[1],
                                device_id=target, device_id_type=MESH,
                            ).start()

        def collect(self, out):
            u = self.u
            waiter(fin.at[u, self.t], self.sem(4)[1]).wait()
            for q in range(4):

                @pl.when(quarter == q)
                def _():
                    for i in range(self.count):
                        tile = self.first + i
                        out[:, tile * 128 : (tile + 1) * 128] = fin[u, tile].astype(F32)[
                            4 * q : 4 * q + OUT_ROWS
                        ]

        def drain(self):
            u, t = self.u, self.t
            waiter(r1.at[u, t], self.sem(0)[0]).wait()
            waiter(ra.at[u, :, t], self.sem(1)[0]).wait()
            waiter(rb.at[u, :, t], self.sem(2)[0]).wait()

            @pl.when(jnp.logical_not(self.is_root))
            def _():
                waiter(q3.at[u, t], self.sem(3)[0]).wait()

            @pl.when(self.is_root)
            def _():
                waiter(rz.at[u, :, t], self.sem(4)[0]).wait()

                @pl.when(jnp.logical_not(self.own_target))
                def _():
                    waiter(q4.at[u, t], self_send.at[u, self.ch]).wait()

    img_chunks = [Chunk(0, ch) for ch in range(NCH)]
    txt_chunks = [Chunk(1, ch) for ch in range(NCH)]

    def back(delta, proj, staged, out, index):
        for n, wide in COLUMNS:
            staged[:, n : n + wide] = against(delta[...], proj[n : n + wide, :]).astype(BF16)
        copy = pltpu.make_async_copy(staged, out, store_sem.at[index])
        copy.start()
        return copy

    finish(img_grad, img_exact, img_inv, img_delta)
    for chunk in img_chunks:
        chunk.make(img_feat, img_delta)
    for chunk in img_chunks:
        chunk.add_core()
    img_store = back(img_delta, img_proj, img_back, img_back_hbm, 0)

    for h in range(2):
        for index in range(h * HALF // MSG, (h + 1) * HALF // MSG):
            img_direct(index).wait_recv()

            @pl.when(c == 0)
            def _():
                img_aside(img_dir, index).start()

        pair_img(img_dir, pos_dir, h * HALF, HALF)

        @pl.when(c == 1)
        def _():
            side_img(h * HALF, HALF)

        if h == 0:
            for chunk in img_chunks:
                chunk.add_near()

    finish(txt_grad, txt_exact, txt_inv, txt_delta)
    for chunk in txt_chunks:
        chunk.make(txt_feat, txt_delta)
    for chunk in txt_chunks:
        chunk.add_core()
    for chunk in img_chunks:
        chunk.add_far()
    txt_store = back(txt_delta, txt_proj, txt_back, txt_back_hbm, 1)
    txt_chunks[0].add_near()
    for chunk in img_chunks:
        chunk.add_z()
    txt_chunks[1].add_near()
    txt_chunks[2].add_near()
    txt_chunks[0].add_far()
    txt_chunks[3].add_near()
    txt_chunks[1].add_far()
    txt_chunks[4].add_near()
    for chunk in txt_chunks[2:]:
        chunk.add_far()
    for chunk in img_chunks:
        chunk.collect(img_out)
    for chunk in txt_chunks:
        chunk.add_z()
    for chunk in txt_chunks:
        chunk.collect(txt_out)

    img_store.wait()
    txt_store.wait()
    for chunk in img_chunks + txt_chunks:
        chunk.drain()
    for index in range(NMSG):
        img_direct(index).wait_send()
        txt_aside(txt_own, index).wait_send()
        img_aside(img_own, index).wait_send()
    pos_ahead.wait_send()
    pos_aside(pos).wait_send()


def deliver(*refs):
    sources, targets, held, load_sem, store_sem = refs[:4], refs[4:8], refs[8:12], refs[12], refs[13]
    places = [(i, pl.ds(row, 128)) for i in range(2) for row in range(0, ROWS, 128)]
    places += [(i, slice(None)) for i in (2, 3)]
    loads, stores = [], []
    for n, (i, at) in enumerate(places):
        here = held[i].at[at]
        loads.append(pltpu.make_async_copy(sources[i].at[at], here, load_sem.at[n]))
        stores.append(pltpu.make_async_copy(here, targets[i].at[at], store_sem.at[n]))
    for load in loads:
        load.start()
    for load, store in zip(loads, stores):
        load.wait()
        store.start()
    for store in stores:
        store.wait()


def per_device(img_feat, txt_feat, img_proj, txt_proj, pos_index, logit_scale, logit_bias):
    pos = pos_index.reshape(4, 128)
    anywhere = pl.BlockSpec(memory_space=pl.ANY)
    scalar = pl.BlockSpec(memory_space=pltpu.SMEM)
    vmem = pl.BlockSpec(memory_space=pltpu.VMEM)
    block16 = pltpu.VMEM((ROWS, WIDTH), BF16)
    block32 = pltpu.VMEM((ROWS, WIDTH), F32)
    square = pltpu.VMEM((WIDTH, WIDTH), BF16)
    places = pltpu.VMEM((4, 128), jnp.int32)
    dma = pltpu.SemaphoreType.DMA
    results = pl.pallas_call(
        kernel,
        name="pairwise",
        out_shape=(
            jax.ShapeDtypeStruct((ROWS, WIDTH), BF16),
            jax.ShapeDtypeStruct((ROWS, WIDTH), BF16),
            jax.ShapeDtypeStruct((OUT_ROWS, WIDTH), F32),
            jax.ShapeDtypeStruct((OUT_ROWS, WIDTH), F32),
        ),
        in_specs=[anywhere] * 5 + [scalar] * 2,
        out_specs=(anywhere, anywhere, vmem, vmem),
        scratch_shapes=[
            block16, block16, square, square, places,
            block16, block16, block16, block16, block16, block16, places, places,
            pltpu.VMEM((ROWS, HALF), jnp.int32),
            block32, block32, pltpu.VMEM((ROWS, 1), F32), pltpu.VMEM((ROWS, 1), F32),
            block32, block32, pltpu.VMEM((ROWS, ROWS), BF16),
            block16, block16, block16, block16,
            pltpu.VMEM((2, TILES, WIDTH, 128), BF16),
            pltpu.VMEM((2, TILES, WIDTH // 2, 128), BF16),
            pltpu.VMEM((2, 3, TILES, ZROWS, 128), BF16),
            pltpu.VMEM((2, TILES, ZROWS, 128), BF16),
            pltpu.VMEM((2, 3, TILES, WIN, 128), BF16),
            pltpu.VMEM((2, TILES, WIN, 128), BF16),
            pltpu.VMEM((2, 7, TILES, WIN, 128), BF16),
            pltpu.VMEM((2, TILES, WIN, 128), BF16),
            pltpu.VMEM((2, TILES, WIN, 128), BF16),
            dma((5,)), dma((2,)),
            dma((NMSG,)), dma((NMSG,)), dma((NMSG,)), dma((NMSG,)),
            dma((NMSG,)), dma((NMSG,)), dma((NMSG,)), dma((NMSG,)),
            dma((2,)), dma((2,)),
            dma((2, NCH, 5)), dma((2, NCH, 5)), dma((2, NCH)),
            pltpu.SemaphoreType.REGULAR,
        ],
        compiler_params=pltpu.CompilerParams(
            collective_id=0, has_side_effects=True, vmem_limit_bytes=62 * 1024 * 1024
        ),
        cost_estimate=pl.CostEstimate(
            flops=15_000_000_000, bytes_accessed=12_000_000, transcendentals=1_500_000
        ),
    )(img_feat, txt_feat, img_proj, txt_proj, pos, logit_scale, logit_bias)
    return pl.pallas_call(
        deliver,
        name="deliver",
        out_shape=tuple(jax.ShapeDtypeStruct(item.shape, item.dtype) for item in results),
        in_specs=[anywhere] * 4,
        out_specs=(anywhere,) * 4,
        scratch_shapes=[pltpu.VMEM(item.shape, item.dtype) for item in results]
        + [dma((10,)), dma((10,))],
    )(*results)


def solution(mesh):
    both = P(("group", "blk"), None)
    in_specs = (both, both, P(), P(), P(("group", "blk")), P(), P())
    out_specs = (both, both, P("blk", None), P("blk", None))
    return jax.shard_map(
        per_device, mesh=mesh, in_specs=in_specs, out_specs=out_specs, check_vma=False
    )
```

```python
import functools

import jax
import jax.numpy as jnp
from jax import lax
from jax.experimental import pallas as pl
from jax.experimental.pallas import tpu as pltpu
from jax.sharding import PartitionSpec as P

MESH = pl.DeviceIdType.MESH
EPSILON = 1e-06
ROWS = 512
WIDTH = 1152
HALF = 256
STEP = 128
MSG = 64
NMSG = ROWS // MSG
PER_STEP = STEP // MSG
TILES = WIDTH // 128
CHUNKS = (((0, 3), (3, 3), (6, 3)), ((0, 2), (2, 2), (4, 2), (6, 2), (8, 1)))
ORDERS = ("x", "m")
COLUMNS = tuple((n, min(256, WIDTH - n)) for n in range(0, WIDTH, 256))
NCH = 5
ZROWS = 144
WIN = 48
OUT_ROWS = 36
BF16 = jnp.bfloat16
F32 = jnp.float32


def against(left, right):
    return lax.dot_general(
        left, right, (((1,), (1,)), ((), ())), preferred_element_type=F32
    )


def kernel(
    img_feat_hbm, txt_feat_hbm, img_proj_hbm, txt_proj_hbm, pos_hbm, scale_ref, bias_ref,
    img_back_hbm, txt_back_hbm, img_out, txt_out,
    img_feat, txt_feat, img_proj, txt_proj, pos,
    img_own, txt_own, img_in, txt_dir, txt_side, pos_dir, pos_side, pos_rows,
    img_exact, txt_exact, img_inv, txt_inv, img_grad, txt_grad, weights,
    img_delta, txt_delta, img_back, txt_back,
    part, r1, ra, q2, rb, q3, rz, q4, fin,
    load_sem, store_sem,
    ts_send, ts_recv, td_send, td_recv, is_send, is_recv, id_send, id_recv, pos_send, pos_recv,
    rs_send, rs_recv, self_send, turn_sem,
):
    group = lax.axis_index("group")
    blk = lax.axis_index("blk")
    x, y_lo = group // 2, lax.rem(group, 2)
    z, y_hi, c = blk // 4, lax.rem(blk // 2, 2), lax.rem(blk, 2)
    y = 2 * y_hi + y_lo
    quarter = 2 * y_hi + c

    def device(x, y, z, c):
        return (x * 2 + lax.rem(y, 2), z * 4 + (y // 2) * 2 + c)

    following = (group, lax.rem(blk + 2, 32))
    previous = (group, lax.rem(blk + 30, 32))
    sibling = (group, blk + 1 - 2 * c)
    root_z = {"x": x + 4 * c, "y": y + 4 * c}
    is_root = {order: z == root_z[order] for order in "xy"}
    window = {"x": y, "y": x}
    own_target = {
        order: (y_hi == window[order] // 2) & (c == lax.rem(window[order], 2)) for order in "xy"
    }

    def x_peer(d):
        return lax.rem(x + d, 4)

    def y_peer(d):
        return lax.rem(y + d, 4)

    def load(index, src, dst):
        return pltpu.make_async_copy(src, dst, load_sem.at[index])

    loads = [
        load(0, txt_proj_hbm, txt_proj),
        load(1, txt_feat_hbm, txt_feat),
        load(2, img_proj_hbm, img_proj),
        load(3, img_feat_hbm, img_feat),
        load(4, pos_hbm, pos),
    ]
    for item in loads[:2]:
        item.start()

    barrier = pltpu.get_barrier_semaphore()

    def greet(target):
        pl.semaphore_signal(barrier, inc=1, device_id=target, device_id_type=MESH)

    greet(following)
    greet(previous)
    greet(sibling)
    for d in range(1, 4):
        greet(device(x_peer(d), y, z, c))
        greet(device(x, y_peer(d), z, c))
    sources = {
        "x": device(lax.rem(z, 4), quarter, z, z // 4),
        "y": device(quarter, lax.rem(z, 4), z, z // 4),
    }
    count = 9
    for order in "xy":
        source = sources[order]

        @pl.when((source[0] != group) | (source[1] != blk))
        def _():
            greet(source)

        @pl.when(is_root[order])
        def _():
            for d in range(1, 8):
                greet(device(x, y, lax.rem(z + d, 8), c))

        count = count + jnp.where(is_root[order], 8 - jnp.where(own_target[order], 1, 0), 1)

    scale = scale_ref[0]
    bias = bias_ref[0]

    def embed(feat, proj, exact, own, inv, start):
        for n, wide in COLUMNS:
            exact[start : start + STEP, n : n + wide] = jnp.dot(
                feat[start : start + STEP, :], proj[:, n : n + wide], preferred_element_type=F32
            )
        for i in range(STEP // 64):
            at = pl.ds(start + i * 64, 64)
            value = exact[at, :]
            inverse = lax.rsqrt(jnp.sum(value * value, axis=-1, keepdims=True) + EPSILON)
            unit = value * inverse
            exact[at, :] = unit
            own[at, :] = unit.astype(BF16)
            inv[at, :] = inverse

    def message(src, dst, send, recv, index, target, shift=0):
        return pltpu.make_async_remote_copy(
            src.at[pl.ds(index * MSG, MSG)], dst.at[pl.ds(index * MSG + shift, MSG)],
            send.at[index], recv.at[index], device_id=target, device_id_type=MESH,
        )

    def txt_direct(index):
        return message(txt_own, txt_dir, td_send, td_recv, index, following)

    def txt_aside(src, index):
        return message(src, txt_side, ts_send, ts_recv, index, sibling)

    def img_direct(index):
        return message(img_own, img_in, id_send, id_recv, index, previous)

    def img_aside(src, index):
        shift = 128 if index * MSG >= ROWS - STEP else ROWS + STEP
        return message(src, img_in, is_send, is_recv, index, sibling, shift)

    loads[0].wait()
    loads[1].wait()
    for item in loads[2:]:
        item.start()
    for step in range(ROWS // STEP):
        embed(txt_feat, txt_proj, txt_exact, txt_own, txt_inv, step * STEP)
        if step == 0:
            pl.semaphore_wait(barrier, count)
        for index in range(step * PER_STEP, (step + 1) * PER_STEP):
            txt_direct(index).start()

            @pl.when(c == 0)
            def _():
                txt_aside(txt_own, index).start()

    loads[4].wait()
    pos_ahead = pltpu.make_async_remote_copy(
        pos, pos_dir, pos_send.at[0], pos_recv.at[0], device_id=previous, device_id_type=MESH
    )
    pos_ahead.start()

    def pos_aside(src):
        return pltpu.make_async_remote_copy(
            src, pos_side, pos_send.at[1], pos_recv.at[1], device_id=sibling, device_id_type=MESH
        )

    @pl.when(c == 1)
    def _():
        pos_aside(pos).start()

    loads[2].wait()
    loads[3].wait()
    for step in range(ROWS // STEP):
        embed(img_feat, img_proj, img_exact, img_own, img_inv, step * STEP)

    @pl.when(c == 1)
    def _():
        for index in range(NMSG):
            img_aside(img_own, index).start()

    def pos_row(pos_ref, first, many):
        return jnp.concatenate([pos_ref[first + i : first + i + 1, :] for i in range(many)], axis=1)

    for h in range(2):
        row = jnp.broadcast_to(pos_row(pos, 2 * h, 2), (HALF, HALF))
        pos_rows[pl.ds(h * HALF, HALF), :] = row.T

    def pair(own, other, grad, matches, start, many, fresh=False):
        logits = scale * against(own[...], other[start : start + many, :]) + bias
        weight = jax.nn.sigmoid(logits) - matches(start, many).astype(F32)
        weights[:, :many] = weight.astype(BF16)
        for n, wide in COLUMNS:
            product = jnp.dot(
                weights[:, :many], other[start : start + many, n : n + wide],
                preferred_element_type=F32,
            )
            if fresh:
                grad[:, n : n + wide] = product
            else:
                grad[:, n : n + wide] += product

    def txt_matches(back):
        owner = lax.rem(blk - back + 32, 32)

        def matches(start, many):
            first = owner * ROWS + start
            column = first + lax.broadcasted_iota(jnp.int32, (ROWS, many), 1)
            mine = pos_rows[...]
            if many > HALF:
                mine = jnp.concatenate([mine, mine], axis=1)
            return mine == column

        return matches

    def img_matches(pieces):
        def matches(start, many):
            row = blk * ROWS + lax.broadcasted_iota(jnp.int32, (ROWS, many), 0)
            mine = jnp.concatenate([ref[i : i + 1, :] for ref, i in pieces], axis=1)
            return jnp.broadcast_to(mine, (ROWS, many)) == row

        return matches

    def pair_txt(other, back, start, many, fresh=False):
        pair(img_own, other, img_grad, txt_matches(back), start, many, fresh)

    def pair_img(other, pieces, start, fresh=False):
        pair(txt_own, other, txt_grad, img_matches(pieces), start, 128 * len(pieces), fresh)

    pair_txt(txt_own, 0, 0, ROWS, fresh=True)
    pair_img(img_own, [(pos, i) for i in range(4)], 0, fresh=True)

    pos_ahead.wait_recv()

    @pl.when(c == 0)
    def _():
        pos_aside(pos_dir).start()

    pos_aside(pos).wait_recv()

    def side_txt(start, many):
        for index in range(start // MSG, (start + many) // MSG):
            txt_aside(txt_own, index).wait_recv()
        pair_txt(txt_side, 1, start, many)

    def wait_aside(indices):
        for index in indices:
            img_aside(img_own, index).wait_recv()

    @pl.when(c == 1)
    def _():
        side_txt(0, ROWS)

    @pl.when(c == 0)
    def _():
        wait_aside(range(NMSG))
        pair_img(img_in, [(pos_side, i) for i in (3, 0, 1, 2)], ROWS)

    for h in range(2):
        for index in range(h * HALF // MSG, (h + 1) * HALF // MSG):
            txt_direct(index).wait_recv()

            @pl.when(c == 1)
            def _():
                txt_aside(txt_dir, index).start()

            txt_direct(index).wait_send()
            if index == NMSG - 2:
                for d in range(1, 4):
                    pl.semaphore_signal(
                        turn_sem, inc=1, device_id=device(x, y_peer(d), z, c), device_id_type=MESH
                    )
                pl.semaphore_signal(turn_sem, inc=1, device_id=sibling, device_id_type=MESH)

        if h == 1:
            pl.semaphore_wait(turn_sem, 4)
            for index in range(NMSG):
                img_direct(index).start()
        pair_txt(txt_dir, 2, h * HALF, HALF)

        @pl.when(c == 0)
        def _():
            side_txt(h * HALF, HALF)

    def finish(grad, exact, inv, delta):
        def rows(i, _):
            for j in range(4):
                at = pl.ds(pl.multiple_of(i * 128 + j * 32, 32), 32)
                value = scale * grad[at, :]
                unit = exact[at, :]
                along = jnp.sum(unit * value, axis=-1, keepdims=True)
                delta[at, :] = (inv[at, :] * (value - unit * along)).astype(BF16)
            return 0

        lax.fori_loop(0, ROWS // 128, rows, 0)

    def waiter(ref, sem):
        return pltpu.make_async_copy(ref, ref, sem)

    class Chunk:
        def __init__(self, u, ch):
            self.u, self.ch = u, ch
            first, count = CHUNKS[u][ch]
            self.t = pl.ds(first, count)
            self.first, self.count = first, count
            order = ORDERS[u]
            self.along_x = (c == 0) if order == "m" else (c >= 0)
            self.is_root = self.choose(is_root["x"], is_root["y"])
            self.own_target = self.choose(own_target["x"], own_target["y"])
            self.root_z = self.choose(root_z["x"], root_z["y"])
            self.near, self.far = self.choose(x, y), self.choose(y, x)

        def choose(self, if_x, if_y):
            if if_x.dtype == jnp.bool_:
                return (self.along_x & if_x) | (jnp.logical_not(self.along_x) & if_y)
            return jnp.where(self.along_x, if_x, if_y)

        def near_peer(self, d):
            target = device(self.choose(x_peer(d), x), self.choose(y, y_peer(d)), z, c)
            return self.choose(x_peer(d), y_peer(d)), target

        def far_peer(self, d):
            target = device(self.choose(x, x_peer(d)), self.choose(y_peer(d), y), z, c)
            return self.choose(y_peer(d), x_peer(d)), target

        def sem(self, stage):
            return rs_send.at[self.u, self.ch, stage], rs_recv.at[self.u, self.ch, stage]

        def copy(self, stage, src, dst, target):
            send, recv = self.sem(stage)
            pltpu.make_async_remote_copy(
                src, dst, send, recv, device_id=target, device_id_type=MESH
            ).start()

        def make(self, feat, delta):
            columns = pl.ds(self.first * 128, self.count * 128)
            value = lax.dot_general(
                feat[...], delta[:, columns], (((0,), (0,)), ((), ())),
                preferred_element_type=F32,
            ).astype(BF16)
            for i in range(self.count):
                part[self.u, self.first + i] = value[:, i * 128 : (i + 1) * 128]
            other = pl.ds(pl.multiple_of(576 * (1 - c), 576), 576)
            self.copy(0, part.at[self.u, self.t, other], r1.at[self.u, self.t], sibling)

        def add_core(self):
            u, t = self.u, self.t
            send, recv = self.sem(0)
            waiter(r1.at[u, t], recv).wait()

            def step(i, _):
                tile = self.first + i
                mine = pl.ds(pl.multiple_of(576 * c, 576), 576)
                r1[u, tile] = part[u, tile, mine, :] + r1[u, tile]
                return 0

            lax.fori_loop(0, self.count, step, 0)
            for d in range(1, 4):
                place, target = self.near_peer(d)
                rows = pl.ds(pl.multiple_of(ZROWS * place, ZROWS), ZROWS)
                self.copy(1, r1.at[u, t, rows], ra.at[u, d - 1, t], target)

        def add_near(self):
            u, t = self.u, self.t
            waiter(ra.at[u, :, t], self.sem(1)[1]).wait()

            def step(i, _):
                tile = self.first + i
                rows = pl.ds(pl.multiple_of(ZROWS * self.near, ZROWS), ZROWS)
                total = r1[u, tile, rows, :].astype(F32)
                for d in range(3):
                    total = total + ra[u, d, tile].astype(F32)
                q2[u, tile] = total.astype(BF16)
                return 0

            lax.fori_loop(0, self.count, step, 0)
            for d in range(1, 4):
                place, target = self.far_peer(d)
                rows = pl.ds(pl.multiple_of(32 * place, 32), WIN)
                self.copy(2, q2.at[u, t, rows], rb.at[u, d - 1, t], target)

        def add_far(self):
            u, t = self.u, self.t
            waiter(rb.at[u, :, t], self.sem(2)[1]).wait()

            def step(i, _):
                tile = self.first + i
                rows = pl.ds(pl.multiple_of(32 * self.far, 32), WIN)
                total = q2[u, tile, rows, :].astype(F32)
                for d in range(3):
                    total = total + rb[u, d, tile].astype(F32)
                q3[u, tile] = total.astype(BF16)
                return 0

            lax.fori_loop(0, self.count, step, 0)

            @pl.when(jnp.logical_not(self.is_root))
            def _():
                far_z = self.root_z
                slot = lax.rem(z - far_z + 8, 8) - 1
                self.copy(3, q3.at[u, t], rz.at[u, slot, t], device(x, y, far_z, c))

        def targets(self):
            for dx in range(4):
                for dy in range(2):
                    far_y = 2 * (self.far // 2) + lax.rem(y_lo + dy, 2)
                    yield (dx, dy), device(x_peer(dx), far_y, z, lax.rem(self.far, 2))

        def add_z(self):
            u, t = self.u, self.t

            @pl.when(self.is_root)
            def _():
                waiter(rz.at[u, :, t], self.sem(3)[1]).wait()

                def step(i, _):
                    tile = self.first + i
                    total = q3[u, tile].astype(F32)
                    for d in range(7):
                        total = total + rz[u, d, tile].astype(F32)
                    q4[u, tile] = total.astype(BF16)
                    return 0

                lax.fori_loop(0, self.count, step, 0)
                for where, target in self.targets():
                    if where != (0, 0):
                        self.copy(4, q4.at[u, t], fin.at[u, t], target)
                    else:

                        @pl.when(self.own_target)
                        def _():
                            pltpu.make_async_copy(
                                q4.at[u, t], fin.at[u, t], self.sem(4)[1]
                            ).start()

                        @pl.when(jnp.logical_not(self.own_target))
                        def _():
                            pltpu.make_async_remote_copy(
                                q4.at[u, t], fin.at[u, t],
                                self_send.at[u, self.ch], self.sem(4)[1],
                                device_id=target, device_id_type=MESH,
                            ).start()

        def collect(self, out):
            u = self.u
            waiter(fin.at[u, self.t], self.sem(4)[1]).wait()
            for q in range(4):

                @pl.when(quarter == q)
                def _():
                    for i in range(self.count):
                        tile = self.first + i
                        out[:, tile * 128 : (tile + 1) * 128] = fin[u, tile].astype(F32)[
                            4 * q : 4 * q + OUT_ROWS
                        ]

        def drain(self):
            u, t = self.u, self.t
            waiter(r1.at[u, t], self.sem(0)[0]).wait()
            waiter(ra.at[u, :, t], self.sem(1)[0]).wait()
            waiter(rb.at[u, :, t], self.sem(2)[0]).wait()

            @pl.when(jnp.logical_not(self.is_root))
            def _():
                waiter(q3.at[u, t], self.sem(3)[0]).wait()

            @pl.when(self.is_root)
            def _():
                waiter(rz.at[u, :, t], self.sem(4)[0]).wait()

                @pl.when(jnp.logical_not(self.own_target))
                def _():
                    waiter(q4.at[u, t], self_send.at[u, self.ch]).wait()

    img_chunks, txt_chunks = ([Chunk(u, ch) for ch in range(len(CHUNKS[u]))] for u in range(2))

    def back(delta, proj, staged, out, index):
        for n, wide in COLUMNS:
            staged[:, n : n + wide] = against(delta[...], proj[n : n + wide, :]).astype(BF16)
        copy = pltpu.make_async_copy(staged, out, store_sem.at[index])
        copy.start()
        return copy

    finish(img_grad, img_exact, img_inv, img_delta)
    for chunk in img_chunks:
        chunk.make(img_feat, img_delta)
    for chunk in img_chunks:
        chunk.add_core()
    img_store = back(img_delta, img_proj, img_back, img_back_hbm, 0)

    def receive(indices):
        for index in indices:
            img_direct(index).wait_recv()

            @pl.when(c == 0)
            def _():
                img_aside(img_in, index).start()

    receive(range(0, 4))
    pair_img(img_in, [(pos_dir, 0), (pos_dir, 1)], 0)

    @pl.when(c == 1)
    def _():
        wait_aside(range(0, 4))
        pair_img(img_in, [(pos_side, 0), (pos_side, 1)], ROWS + STEP)

    for chunk in img_chunks:
        chunk.add_near()
    receive((4, 5))

    @pl.when(c == 1)
    def _():
        pair_img(img_in, [(pos_dir, 2)], HALF)
        wait_aside((4, 5))
        pair_img(img_in, [(pos_side, 2)], 2 * ROWS - STEP)

    receive((6, 7))

    @pl.when(c == 0)
    def _():
        pair_img(img_in, [(pos_dir, 2), (pos_dir, 3)], HALF)

    @pl.when(c == 1)
    def _():
        wait_aside((6, 7))
        pair_img(img_in, [(pos_dir, 3), (pos_side, 3)], ROWS - STEP)

    finish(txt_grad, txt_exact, txt_inv, txt_delta)
    for chunk in txt_chunks:
        chunk.make(txt_feat, txt_delta)
    for chunk in txt_chunks:
        chunk.add_core()
    for chunk in img_chunks:
        chunk.add_far()
    txt_store = back(txt_delta, txt_proj, txt_back, txt_back_hbm, 1)
    txt_chunks[0].add_near()
    for chunk in img_chunks:
        chunk.add_z()
    txt_chunks[1].add_near()
    txt_chunks[2].add_near()
    txt_chunks[0].add_far()
    txt_chunks[3].add_near()
    txt_chunks[1].add_far()
    txt_chunks[4].add_near()
    for chunk in txt_chunks[2:]:
        chunk.add_far()
    for chunk in img_chunks:
        chunk.collect(img_out)
    for chunk in txt_chunks:
        chunk.add_z()
    for chunk in txt_chunks:
        chunk.collect(txt_out)

    img_store.wait()
    txt_store.wait()
    for chunk in img_chunks + txt_chunks:
        chunk.drain()
    for index in range(NMSG):
        img_direct(index).wait_send()
        txt_aside(txt_own, index).wait_send()
        img_aside(img_own, index).wait_send()
    pos_ahead.wait_send()
    pos_aside(pos).wait_send()


def deliver(*refs):
    sources, targets, held, load_sem, store_sem = refs[:4], refs[4:8], refs[8:12], refs[12], refs[13]
    places = [(i, pl.ds(row, 128)) for i in range(2) for row in range(0, ROWS, 128)]
    places += [(i, slice(None)) for i in (2, 3)]
    loads, stores = [], []
    for n, (i, at) in enumerate(places):
        here = held[i].at[at]
        loads.append(pltpu.make_async_copy(sources[i].at[at], here, load_sem.at[n]))
        stores.append(pltpu.make_async_copy(here, targets[i].at[at], store_sem.at[n]))
    for load in loads:
        load.start()
    for load, store in zip(loads, stores):
        load.wait()
        store.start()
    for store in stores:
        store.wait()


def per_device(img_feat, txt_feat, img_proj, txt_proj, pos_index, logit_scale, logit_bias):
    pos = pos_index.reshape(4, 128)
    anywhere = pl.BlockSpec(memory_space=pl.ANY)
    scalar = pl.BlockSpec(memory_space=pltpu.SMEM)
    vmem = pl.BlockSpec(memory_space=pltpu.VMEM)
    block16 = pltpu.VMEM((ROWS, WIDTH), BF16)
    block32 = pltpu.VMEM((ROWS, WIDTH), F32)
    square = pltpu.VMEM((WIDTH, WIDTH), BF16)
    places = pltpu.VMEM((4, 128), jnp.int32)
    dma = pltpu.SemaphoreType.DMA
    results = pl.pallas_call(
        kernel,
        name="pairwise",
        out_shape=(
            jax.ShapeDtypeStruct((ROWS, WIDTH), BF16),
            jax.ShapeDtypeStruct((ROWS, WIDTH), BF16),
            jax.ShapeDtypeStruct((OUT_ROWS, WIDTH), F32),
            jax.ShapeDtypeStruct((OUT_ROWS, WIDTH), F32),
        ),
        in_specs=[anywhere] * 5 + [scalar] * 2,
        out_specs=(anywhere, anywhere, vmem, vmem),
        scratch_shapes=[
            block16, block16, square, square, places,
            block16, block16, pltpu.VMEM((2 * ROWS, WIDTH), BF16), block16, block16, places, places,
            pltpu.VMEM((ROWS, HALF), jnp.int32),
            block32, block32, pltpu.VMEM((ROWS, 1), F32), pltpu.VMEM((ROWS, 1), F32),
            block32, block32, pltpu.VMEM((ROWS, ROWS), BF16),
            block16, block16, block16, block16,
            pltpu.VMEM((2, TILES, WIDTH, 128), BF16),
            pltpu.VMEM((2, TILES, WIDTH // 2, 128), BF16),
            pltpu.VMEM((2, 3, TILES, ZROWS, 128), BF16),
            pltpu.VMEM((2, TILES, ZROWS, 128), BF16),
            pltpu.VMEM((2, 3, TILES, WIN, 128), BF16),
            pltpu.VMEM((2, TILES, WIN, 128), BF16),
            pltpu.VMEM((2, 7, TILES, WIN, 128), BF16),
            pltpu.VMEM((2, TILES, WIN, 128), BF16),
            pltpu.VMEM((2, TILES, WIN, 128), BF16),
            dma((5,)), dma((2,)),
            dma((NMSG,)), dma((NMSG,)), dma((NMSG,)), dma((NMSG,)),
            dma((NMSG,)), dma((NMSG,)), dma((NMSG,)), dma((NMSG,)),
            dma((2,)), dma((2,)),
            dma((2, NCH, 5)), dma((2, NCH, 5)), dma((2, NCH)),
            pltpu.SemaphoreType.REGULAR,
        ],
        compiler_params=pltpu.CompilerParams(
            collective_id=0, has_side_effects=True, vmem_limit_bytes=62 * 1024 * 1024
        ),
        cost_estimate=pl.CostEstimate(
            flops=15_000_000_000, bytes_accessed=12_000_000, transcendentals=1_500_000
        ),
    )(img_feat, txt_feat, img_proj, txt_proj, pos, logit_scale, logit_bias)
    return pl.pallas_call(
        deliver,
        name="deliver",
        out_shape=tuple(jax.ShapeDtypeStruct(item.shape, item.dtype) for item in results),
        in_specs=[anywhere] * 4,
        out_specs=(anywhere,) * 4,
        scratch_shapes=[pltpu.VMEM(item.shape, item.dtype) for item in results]
        + [dma((10,)), dma((10,))],
    )(*results)


def solution(mesh):
    both = P(("group", "blk"), None)
    in_specs = (both, both, P(), P(), P(("group", "blk")), P(), P())
    out_specs = (both, both, P("blk", None), P("blk", None))
    return jax.shard_map(
        per_device, mesh=mesh, in_specs=in_specs, out_specs=out_specs, check_vma=False
    )
```

```python
import functools

import jax
import jax.numpy as jnp
from jax import lax
from jax.experimental import pallas as pl
from jax.experimental.pallas import tpu as pltpu
from jax.sharding import PartitionSpec as P

MESH = pl.DeviceIdType.MESH
EPSILON = 1e-06
ROWS = 512
WIDTH = 1152
HALF = 256
STEP = 128
MSG = 64
NMSG = ROWS // MSG
PER_STEP = STEP // MSG
TILES = WIDTH // 128
CHUNKS = (((0, 3), (3, 3), (6, 3)), ((0, 2), (2, 2), (4, 4), (8, 1)))
ORDERS = ("x", "m")
COLUMNS = tuple((n, min(256, WIDTH - n)) for n in range(0, WIDTH, 256))
NCH = 5
ZROWS = 144
WIN = 48
OUT_ROWS = 36
BF16 = jnp.bfloat16
F32 = jnp.float32


def against(left, right):
    return lax.dot_general(
        left, right, (((1,), (1,)), ((), ())), preferred_element_type=F32
    )


def kernel(
    img_feat_hbm, txt_feat_hbm, img_proj_hbm, txt_proj_hbm, pos_hbm, scale_ref, bias_ref,
    img_back_hbm, txt_back_hbm, img_out, txt_out,
    img_feat, txt_feat, img_proj, txt_proj, pos,
    img_own, txt_own, img_in, txt_dir, txt_side, pos_dir, pos_side, pos_rows,
    img_exact, txt_exact, img_inv, txt_inv, img_grad, txt_grad, weights,
    img_delta, txt_delta, img_back, txt_back,
    part, r1, ra, q2, rb, q3, rz, q4, fin,
    load_sem, store_sem,
    ts_send, ts_recv, td_send, td_recv, is_send, is_recv, id_send, id_recv, pos_send, pos_recv,
    rs_send, rs_recv, self_send, turn_sem,
):
    group = lax.axis_index("group")
    blk = lax.axis_index("blk")
    x, y_lo = group // 2, lax.rem(group, 2)
    z, y_hi, c = blk // 4, lax.rem(blk // 2, 2), lax.rem(blk, 2)
    y = 2 * y_hi + y_lo
    quarter = 2 * y_hi + c

    def device(x, y, z, c):
        return (x * 2 + lax.rem(y, 2), z * 4 + (y // 2) * 2 + c)

    following = (group, lax.rem(blk + 2, 32))
    previous = (group, lax.rem(blk + 30, 32))
    sibling = (group, blk + 1 - 2 * c)
    root_z = {"x": x + 4 * c, "y": y + 4 * c}
    is_root = {order: z == root_z[order] for order in "xy"}
    window = {"x": y, "y": x}
    own_target = {
        order: (y_hi == window[order] // 2) & (c == lax.rem(window[order], 2)) for order in "xy"
    }

    def x_peer(d):
        return lax.rem(x + d, 4)

    def y_peer(d):
        return lax.rem(y + d, 4)

    def load(index, src, dst):
        return pltpu.make_async_copy(src, dst, load_sem.at[index])

    loads = [
        load(0, txt_proj_hbm, txt_proj),
        load(1, txt_feat_hbm, txt_feat),
        load(2, img_proj_hbm, img_proj),
        load(3, img_feat_hbm, img_feat),
        load(4, pos_hbm, pos),
    ]
    for item in loads[:2]:
        item.start()

    barrier = pltpu.get_barrier_semaphore()

    def greet(target):
        pl.semaphore_signal(barrier, inc=1, device_id=target, device_id_type=MESH)

    greet(following)
    greet(previous)
    greet(sibling)
    for d in range(1, 4):
        greet(device(x_peer(d), y, z, c))
        greet(device(x, y_peer(d), z, c))
    sources = {
        "x": device(lax.rem(z, 4), quarter, z, z // 4),
        "y": device(quarter, lax.rem(z, 4), z, z // 4),
    }
    count = 9
    for order in "xy":
        source = sources[order]

        @pl.when((source[0] != group) | (source[1] != blk))
        def _():
            greet(source)

        @pl.when(is_root[order])
        def _():
            for d in range(1, 8):
                greet(device(x, y, lax.rem(z + d, 8), c))

        count = count + jnp.where(is_root[order], 8 - jnp.where(own_target[order], 1, 0), 1)

    scale = scale_ref[0]
    bias = bias_ref[0]

    def embed(feat, proj, exact, own, inv, start):
        for n, wide in COLUMNS:
            exact[start : start + STEP, n : n + wide] = jnp.dot(
                feat[start : start + STEP, :], proj[:, n : n + wide], preferred_element_type=F32
            )
        for i in range(STEP // 64):
            at = pl.ds(start + i * 64, 64)
            value = exact[at, :]
            inverse = lax.rsqrt(jnp.sum(value * value, axis=-1, keepdims=True) + EPSILON)
            unit = value * inverse
            exact[at, :] = unit
            own[at, :] = unit.astype(BF16)
            inv[at, :] = inverse

    def message(src, dst, send, recv, index, target, shift=0):
        return pltpu.make_async_remote_copy(
            src.at[pl.ds(index * MSG, MSG)], dst.at[pl.ds(index * MSG + shift, MSG)],
            send.at[index], recv.at[index], device_id=target, device_id_type=MESH,
        )

    def txt_direct(index):
        return message(txt_own, txt_dir, td_send, td_recv, index, following)

    def txt_aside(src, index):
        return message(src, txt_side, ts_send, ts_recv, index, sibling)

    def img_direct(index):
        return message(img_own, img_in, id_send, id_recv, index, previous)

    def img_aside(src, index):
        shift = 128 if index * MSG >= ROWS - STEP else ROWS + STEP
        return message(src, img_in, is_send, is_recv, index, sibling, shift)

    loads[0].wait()
    loads[1].wait()
    for item in loads[2:]:
        item.start()
    for step in range(ROWS // STEP):
        embed(txt_feat, txt_proj, txt_exact, txt_own, txt_inv, step * STEP)
        if step == 0:
            pl.semaphore_wait(barrier, count)
        for index in range(step * PER_STEP, (step + 1) * PER_STEP):
            txt_direct(index).start()

            @pl.when(c == 0)
            def _():
                txt_aside(txt_own, index).start()

    loads[4].wait()
    pos_ahead = pltpu.make_async_remote_copy(
        pos, pos_dir, pos_send.at[0], pos_recv.at[0], device_id=previous, device_id_type=MESH
    )
    pos_ahead.start()

    def pos_aside(src):
        return pltpu.make_async_remote_copy(
            src, pos_side, pos_send.at[1], pos_recv.at[1], device_id=sibling, device_id_type=MESH
        )

    @pl.when(c == 1)
    def _():
        pos_aside(pos).start()

    loads[2].wait()
    loads[3].wait()
    for step in range(ROWS // STEP):
        embed(img_feat, img_proj, img_exact, img_own, img_inv, step * STEP)

    @pl.when(c == 1)
    def _():
        for index in range(NMSG):
            img_aside(img_own, index).start()

    def pos_row(pos_ref, first, many):
        return jnp.concatenate([pos_ref[first + i : first + i + 1, :] for i in range(many)], axis=1)

    for h in range(2):
        row = jnp.broadcast_to(pos_row(pos, 2 * h, 2), (HALF, HALF))
        pos_rows[pl.ds(h * HALF, HALF), :] = row.T

    def pair(own, other, grad, matches, start, many, fresh=False):
        logits = scale * against(own[...], other[start : start + many, :]) + bias
        weight = jax.nn.sigmoid(logits) - matches(start, many).astype(F32)
        weights[:, :many] = weight.astype(BF16)
        for n, wide in COLUMNS:
            product = jnp.dot(
                weights[:, :many], other[start : start + many, n : n + wide],
                preferred_element_type=F32,
            )
            if fresh:
                grad[:, n : n + wide] = product
            else:
                grad[:, n : n + wide] += product

    def txt_matches(back):
        owner = lax.rem(blk - back + 32, 32)

        def matches(start, many):
            first = owner * ROWS + start
            column = first + lax.broadcasted_iota(jnp.int32, (ROWS, many), 1)
            mine = pos_rows[...]
            if many > HALF:
                mine = jnp.concatenate([mine, mine], axis=1)
            return mine == column

        return matches

    def img_matches(pieces):
        def matches(start, many):
            row = blk * ROWS + lax.broadcasted_iota(jnp.int32, (ROWS, many), 0)
            mine = jnp.concatenate([ref[i : i + 1, :] for ref, i in pieces], axis=1)
            return jnp.broadcast_to(mine, (ROWS, many)) == row

        return matches

    def pair_txt(other, back, start, many, fresh=False):
        pair(img_own, other, img_grad, txt_matches(back), start, many, fresh)

    def pair_img(other, pieces, start, fresh=False):
        pair(txt_own, other, txt_grad, img_matches(pieces), start, 128 * len(pieces), fresh)

    pair_txt(txt_own, 0, 0, ROWS, fresh=True)
    pair_img(img_own, [(pos, i) for i in range(4)], 0, fresh=True)

    pos_ahead.wait_recv()

    @pl.when(c == 0)
    def _():
        pos_aside(pos_dir).start()

    pos_aside(pos).wait_recv()

    def side_txt(start, many):
        for index in range(start // MSG, (start + many) // MSG):
            txt_aside(txt_own, index).wait_recv()
        pair_txt(txt_side, 1, start, many)

    def wait_aside(indices):
        for index in indices:
            img_aside(img_own, index).wait_recv()

    @pl.when(c == 1)
    def _():
        side_txt(0, ROWS)

    @pl.when(c == 0)
    def _():
        wait_aside(range(NMSG))
        pair_img(img_in, [(pos_side, i) for i in (3, 0, 1, 2)], ROWS)

    for h in range(2):
        for index in range(h * HALF // MSG, (h + 1) * HALF // MSG):
            txt_direct(index).wait_recv()

            @pl.when(c == 1)
            def _():
                txt_aside(txt_dir, index).start()

            txt_direct(index).wait_send()
            if index == NMSG - 2:
                for d in range(1, 4):
                    pl.semaphore_signal(
                        turn_sem, inc=1, device_id=device(x, y_peer(d), z, c), device_id_type=MESH
                    )
                pl.semaphore_signal(turn_sem, inc=1, device_id=sibling, device_id_type=MESH)

        if h == 1:
            pl.semaphore_wait(turn_sem, 4)
            for index in range(NMSG):
                img_direct(index).start()
        pair_txt(txt_dir, 2, h * HALF, HALF)

        @pl.when(c == 0)
        def _():
            side_txt(h * HALF, HALF)

    def finish(grad, exact, inv, delta):
        def rows(i, _):
            for j in range(4):
                at = pl.ds(pl.multiple_of(i * 128 + j * 32, 32), 32)
                value = scale * grad[at, :]
                unit = exact[at, :]
                along = jnp.sum(unit * value, axis=-1, keepdims=True)
                delta[at, :] = (inv[at, :] * (value - unit * along)).astype(BF16)
            return 0

        lax.fori_loop(0, ROWS // 128, rows, 0)

    def waiter(ref, sem):
        return pltpu.make_async_copy(ref, ref, sem)

    class Chunk:
        def __init__(self, u, ch):
            self.u, self.ch = u, ch
            first, count = CHUNKS[u][ch]
            self.t = pl.ds(first, count)
            self.first, self.count = first, count
            order = ORDERS[u]
            self.along_x = (c == 0) if order == "m" else (c >= 0)
            self.is_root = self.choose(is_root["x"], is_root["y"])
            self.own_target = self.choose(own_target["x"], own_target["y"])
            self.root_z = self.choose(root_z["x"], root_z["y"])
            self.near, self.far = self.choose(x, y), self.choose(y, x)

        def choose(self, if_x, if_y):
            if if_x.dtype == jnp.bool_:
                return (self.along_x & if_x) | (jnp.logical_not(self.along_x) & if_y)
            return jnp.where(self.along_x, if_x, if_y)

        def near_peer(self, d):
            target = device(self.choose(x_peer(d), x), self.choose(y, y_peer(d)), z, c)
            return self.choose(x_peer(d), y_peer(d)), target

        def far_peer(self, d):
            target = device(self.choose(x, x_peer(d)), self.choose(y_peer(d), y), z, c)
            return self.choose(y_peer(d), x_peer(d)), target

        def sem(self, stage):
            return rs_send.at[self.u, self.ch, stage], rs_recv.at[self.u, self.ch, stage]

        def copy(self, stage, src, dst, target):
            send, recv = self.sem(stage)
            pltpu.make_async_remote_copy(
                src, dst, send, recv, device_id=target, device_id_type=MESH
            ).start()

        def make(self, feat, delta):
            columns = pl.ds(self.first * 128, self.count * 128)
            value = lax.dot_general(
                feat[...], delta[:, columns], (((0,), (0,)), ((), ())),
                preferred_element_type=F32,
            ).astype(BF16)
            for i in range(self.count):
                part[self.u, self.first + i] = value[:, i * 128 : (i + 1) * 128]
            other = pl.ds(pl.multiple_of(576 * (1 - c), 576), 576)
            self.copy(0, part.at[self.u, self.t, other], r1.at[self.u, self.t], sibling)

        def add_core(self):
            u, t = self.u, self.t
            send, recv = self.sem(0)
            waiter(r1.at[u, t], recv).wait()

            def step(i, _):
                tile = self.first + i
                mine = pl.ds(pl.multiple_of(576 * c, 576), 576)
                r1[u, tile] = part[u, tile, mine, :] + r1[u, tile]
                return 0

            lax.fori_loop(0, self.count, step, 0)
            for d in range(1, 4):
                place, target = self.near_peer(d)
                rows = pl.ds(pl.multiple_of(ZROWS * place, ZROWS), ZROWS)
                self.copy(1, r1.at[u, t, rows], ra.at[u, d - 1, t], target)

        def add_near(self):
            u, t = self.u, self.t
            waiter(ra.at[u, :, t], self.sem(1)[1]).wait()

            def step(i, _):
                tile = self.first + i
                rows = pl.ds(pl.multiple_of(ZROWS * self.near, ZROWS), ZROWS)
                total = r1[u, tile, rows, :].astype(F32)
                for d in range(3):
                    total = total + ra[u, d, tile].astype(F32)
                q2[u, tile] = total.astype(BF16)
                return 0

            lax.fori_loop(0, self.count, step, 0)
            for d in range(1, 4):
                place, target = self.far_peer(d)
                rows = pl.ds(pl.multiple_of(32 * place, 32), WIN)
                self.copy(2, q2.at[u, t, rows], rb.at[u, d - 1, t], target)

        def add_far(self):
            u, t = self.u, self.t
            waiter(rb.at[u, :, t], self.sem(2)[1]).wait()

            def step(i, _):
                tile = self.first + i
                rows = pl.ds(pl.multiple_of(32 * self.far, 32), WIN)
                total = q2[u, tile, rows, :].astype(F32)
                for d in range(3):
                    total = total + rb[u, d, tile].astype(F32)
                q3[u, tile] = total.astype(BF16)
                return 0

            lax.fori_loop(0, self.count, step, 0)

            @pl.when(jnp.logical_not(self.is_root))
            def _():
                far_z = self.root_z
                slot = lax.rem(z - far_z + 8, 8) - 1
                self.copy(3, q3.at[u, t], rz.at[u, slot, t], device(x, y, far_z, c))

        def targets(self):
            for dx in range(4):
                for dy in range(2):
                    far_y = 2 * (self.far // 2) + lax.rem(y_lo + dy, 2)
                    yield (dx, dy), device(x_peer(dx), far_y, z, lax.rem(self.far, 2))

        def add_z(self):
            u, t = self.u, self.t

            @pl.when(self.is_root)
            def _():
                waiter(rz.at[u, :, t], self.sem(3)[1]).wait()

                def step(i, _):
                    tile = self.first + i
                    total = q3[u, tile].astype(F32)
                    for d in range(7):
                        total = total + rz[u, d, tile].astype(F32)
                    q4[u, tile] = total.astype(BF16)
                    return 0

                lax.fori_loop(0, self.count, step, 0)
                for where, target in self.targets():
                    if where != (0, 0):
                        self.copy(4, q4.at[u, t], fin.at[u, t], target)
                    else:

                        @pl.when(self.own_target)
                        def _():
                            pltpu.make_async_copy(
                                q4.at[u, t], fin.at[u, t], self.sem(4)[1]
                            ).start()

                        @pl.when(jnp.logical_not(self.own_target))
                        def _():
                            pltpu.make_async_remote_copy(
                                q4.at[u, t], fin.at[u, t],
                                self_send.at[u, self.ch], self.sem(4)[1],
                                device_id=target, device_id_type=MESH,
                            ).start()

        def collect(self, out):
            u = self.u
            waiter(fin.at[u, self.t], self.sem(4)[1]).wait()
            for q in range(4):

                @pl.when(quarter == q)
                def _():
                    for i in range(self.count):
                        tile = self.first + i
                        out[:, tile * 128 : (tile + 1) * 128] = fin[u, tile].astype(F32)[
                            4 * q : 4 * q + OUT_ROWS
                        ]

        def drain(self):
            u, t = self.u, self.t
            waiter(r1.at[u, t], self.sem(0)[0]).wait()
            waiter(ra.at[u, :, t], self.sem(1)[0]).wait()
            waiter(rb.at[u, :, t], self.sem(2)[0]).wait()

            @pl.when(jnp.logical_not(self.is_root))
            def _():
                waiter(q3.at[u, t], self.sem(3)[0]).wait()

            @pl.when(self.is_root)
            def _():
                waiter(rz.at[u, :, t], self.sem(4)[0]).wait()

                @pl.when(jnp.logical_not(self.own_target))
                def _():
                    waiter(q4.at[u, t], self_send.at[u, self.ch]).wait()

    img_chunks, txt_chunks = ([Chunk(u, ch) for ch in range(len(CHUNKS[u]))] for u in range(2))

    def back(delta, proj, staged, out, index):
        for n, wide in COLUMNS:
            staged[:, n : n + wide] = against(delta[...], proj[n : n + wide, :]).astype(BF16)
        copy = pltpu.make_async_copy(staged, out, store_sem.at[index])
        copy.start()
        return copy

    finish(img_grad, img_exact, img_inv, img_delta)
    for chunk in img_chunks:
        chunk.make(img_feat, img_delta)
    for chunk in img_chunks:
        chunk.add_core()
    img_store = back(img_delta, img_proj, img_back, img_back_hbm, 0)

    def receive(indices):
        for index in indices:
            img_direct(index).wait_recv()

            @pl.when(c == 0)
            def _():
                img_aside(img_in, index).start()

    receive(range(0, 4))
    pair_img(img_in, [(pos_dir, 0), (pos_dir, 1)], 0)

    @pl.when(c == 1)
    def _():
        wait_aside(range(0, 4))
        pair_img(img_in, [(pos_side, 0), (pos_side, 1)], ROWS + STEP)

    for chunk in img_chunks:
        chunk.add_near()
    receive((4, 5))

    @pl.when(c == 1)
    def _():
        pair_img(img_in, [(pos_dir, 2)], HALF)
        wait_aside((4, 5))
        pair_img(img_in, [(pos_side, 2)], 2 * ROWS - STEP)

    receive((6, 7))

    @pl.when(c == 0)
    def _():
        pair_img(img_in, [(pos_dir, 2), (pos_dir, 3)], HALF)

    @pl.when(c == 1)
    def _():
        wait_aside((6, 7))
        pair_img(img_in, [(pos_dir, 3), (pos_side, 3)], ROWS - STEP)

    finish(txt_grad, txt_exact, txt_inv, txt_delta)
    for chunk in txt_chunks:
        chunk.make(txt_feat, txt_delta)
    for chunk in txt_chunks:
        chunk.add_core()
    for chunk in img_chunks:
        chunk.add_far()
    txt_store = back(txt_delta, txt_proj, txt_back, txt_back_hbm, 1)
    txt_chunks[0].add_near()
    for chunk in img_chunks:
        chunk.add_z()
    txt_chunks[1].add_near()
    txt_chunks[0].add_far()
    txt_chunks[2].add_near()
    txt_chunks[1].add_far()
    txt_chunks[3].add_near()
    for chunk in txt_chunks[2:]:
        chunk.add_far()
    for chunk in img_chunks:
        chunk.collect(img_out)
    for chunk in txt_chunks:
        chunk.add_z()
    for chunk in txt_chunks:
        chunk.collect(txt_out)

    img_store.wait()
    txt_store.wait()
    for chunk in img_chunks + txt_chunks:
        chunk.drain()
    for index in range(NMSG):
        img_direct(index).wait_send()
        txt_aside(txt_own, index).wait_send()
        img_aside(img_own, index).wait_send()
    pos_ahead.wait_send()
    pos_aside(pos).wait_send()


def deliver(*refs):
    sources, targets, held, load_sem, store_sem = refs[:4], refs[4:8], refs[8:12], refs[12], refs[13]
    places = [(i, pl.ds(row, 128)) for i in range(2) for row in range(0, ROWS, 128)]
    places += [(i, slice(None)) for i in (2, 3)]
    loads, stores = [], []
    for n, (i, at) in enumerate(places):
        here = held[i].at[at]
        loads.append(pltpu.make_async_copy(sources[i].at[at], here, load_sem.at[n]))
        stores.append(pltpu.make_async_copy(here, targets[i].at[at], store_sem.at[n]))
    for load in loads:
        load.start()
    for load, store in zip(loads, stores):
        load.wait()
        store.start()
    for store in stores:
        store.wait()


def per_device(img_feat, txt_feat, img_proj, txt_proj, pos_index, logit_scale, logit_bias):
    pos = pos_index.reshape(4, 128)
    anywhere = pl.BlockSpec(memory_space=pl.ANY)
    scalar = pl.BlockSpec(memory_space=pltpu.SMEM)
    vmem = pl.BlockSpec(memory_space=pltpu.VMEM)
    block16 = pltpu.VMEM((ROWS, WIDTH), BF16)
    block32 = pltpu.VMEM((ROWS, WIDTH), F32)
    square = pltpu.VMEM((WIDTH, WIDTH), BF16)
    places = pltpu.VMEM((4, 128), jnp.int32)
    dma = pltpu.SemaphoreType.DMA
    results = pl.pallas_call(
        kernel,
        name="pairwise",
        out_shape=(
            jax.ShapeDtypeStruct((ROWS, WIDTH), BF16),
            jax.ShapeDtypeStruct((ROWS, WIDTH), BF16),
            jax.ShapeDtypeStruct((OUT_ROWS, WIDTH), F32),
            jax.ShapeDtypeStruct((OUT_ROWS, WIDTH), F32),
        ),
        in_specs=[anywhere] * 5 + [scalar] * 2,
        out_specs=(anywhere, anywhere, vmem, vmem),
        scratch_shapes=[
            block16, block16, square, square, places,
            block16, block16, pltpu.VMEM((2 * ROWS, WIDTH), BF16), block16, block16, places, places,
            pltpu.VMEM((ROWS, HALF), jnp.int32),
            block32, block32, pltpu.VMEM((ROWS, 1), F32), pltpu.VMEM((ROWS, 1), F32),
            block32, block32, pltpu.VMEM((ROWS, ROWS), BF16),
            block16, block16, block16, block16,
            pltpu.VMEM((2, TILES, WIDTH, 128), BF16),
            pltpu.VMEM((2, TILES, WIDTH // 2, 128), BF16),
            pltpu.VMEM((2, 3, TILES, ZROWS, 128), BF16),
            pltpu.VMEM((2, TILES, ZROWS, 128), BF16),
            pltpu.VMEM((2, 3, TILES, WIN, 128), BF16),
            pltpu.VMEM((2, TILES, WIN, 128), BF16),
            pltpu.VMEM((2, 7, TILES, WIN, 128), BF16),
            pltpu.VMEM((2, TILES, WIN, 128), BF16),
            pltpu.VMEM((2, TILES, WIN, 128), BF16),
            dma((5,)), dma((2,)),
            dma((NMSG,)), dma((NMSG,)), dma((NMSG,)), dma((NMSG,)),
            dma((NMSG,)), dma((NMSG,)), dma((NMSG,)), dma((NMSG,)),
            dma((2,)), dma((2,)),
            dma((2, NCH, 5)), dma((2, NCH, 5)), dma((2, NCH)),
            pltpu.SemaphoreType.REGULAR,
        ],
        compiler_params=pltpu.CompilerParams(
            collective_id=0, has_side_effects=True, vmem_limit_bytes=62 * 1024 * 1024
        ),
        cost_estimate=pl.CostEstimate(
            flops=15_000_000_000, bytes_accessed=12_000_000, transcendentals=1_500_000
        ),
    )(img_feat, txt_feat, img_proj, txt_proj, pos, logit_scale, logit_bias)
    return pl.pallas_call(
        deliver,
        name="deliver",
        out_shape=tuple(jax.ShapeDtypeStruct(item.shape, item.dtype) for item in results),
        in_specs=[anywhere] * 4,
        out_specs=(anywhere,) * 4,
        scratch_shapes=[pltpu.VMEM(item.shape, item.dtype) for item in results]
        + [dma((10,)), dma((10,))],
    )(*results)


def solution(mesh):
    both = P(("group", "blk"), None)
    in_specs = (both, both, P(), P(), P(("group", "blk")), P(), P())
    out_specs = (both, both, P("blk", None), P("blk", None))
    return jax.shard_map(
        per_device, mesh=mesh, in_specs=in_specs, out_specs=out_specs, check_vma=False
    )
```
